512 devices in a mesh: dp: 16 (over y_lo, x), seq: 32 (over z, y_hi, core).
Axes of the slice: x: 4, y: 8 (y_hi: 2, y_lo: 4; y = y_hi * 4 + y_lo), z: 8, core: 2. Of those that a mesh axis runs over, the one named last changes fastest.
Arguments:
- gated_input: bfloat16 [16, 16384, 1024], P('dp', 'seq'), may hold values from -6 to 6
- cotangent: bfloat16 [16, 16384, 1024], P('dp', 'seq'), may hold values from -6 to 6
- lengths: int32 [16, 8], P('dp'), may hold values from 1 to 8192, 16384 in all within a row
- kernel: float32 [9, 1024], replicated, may hold values from -2 to 2
- norm_gain: float32 [1024], replicated, may hold values from 0.5 to 1.5
- out_weight: bfloat16 [1024, 1024], P('seq'), may hold values from -0.1875 to 0.1875
Outputs:
- grad_gated: bfloat16 [16, 16384, 1024], P('dp', 'seq')
- grad_weight: float32 [1024, 1024], P('seq')
- grad_kernel: float32 [9, 1024], replicated
- grad_gain: float32 [1024], replicated
The draws below stay inside these ranges and needn't reach their ends.
Inputs may be any that keep to these rules, and one draw needn't show every extreme that they name: Each row holds the lengths of 8 utterances that fill the stream's 16384 frames exactly; in every row the longest is 8192.
All inputs are finite; a program needn't handle non-finite values.
Results may differ from the reference program's by a relative error of at most 0.0029.
Values may be sent and summed in bfloat16 or wider, within the bound.
A program may use at most 64 MiB of HBM per device.

```python
import math
import jax
import jax.numpy as jnp
import numpy as np
from jax import lax

D = 1024
KW = 9
UTTS = 8
GROUPS = 16
FRAMES = 16384


def shard_levels(stream_key, shape, cuts, smallest, largest):
    def one(dim, blocks):
        steps = jax.random.uniform(jax.random.fold_in(jax.random.fold_in(stream_key, 6), dim), (blocks,), jnp.float32, smallest / len(cuts), largest / len(cuts))
        return jnp.repeat(jnp.exp(steps), shape[dim] // blocks).reshape((-1,) + (1,) * (len(shape) - dim - 1))

    gain = one(*cuts[0])
    for cut in cuts[1:]:
        gain = gain * one(*cut)
    return gain


def length_profile(amount, total, most, skew):
    portions = [(1 << 20) // math.isqrt(standing ** skew) + 1 for standing in range(2, amount + 1)]
    spare, given = total - most - (amount - 1), [1] * (amount - 1)
    while spare > 0:
        movable = [i for i in range(amount - 1) if given[i] < most]
        pool, left = sum([portions[i] for i in movable]), spare
        for i in movable:
            more = min(most - given[i], max(1, left * portions[i] // pool), spare)
            given[i] = given[i] + more
            spare = spare - more
    return np.array([most] + given)


def uneven(key, count, total, bound, skew):
    if count == 2:
        one = jax.random.randint(key, (), max(1, total - bound), min(bound, total - 1) + 1)
        return jnp.stack([one, total - one])
    sizes = jnp.asarray(length_profile(count, total, bound, skew), jnp.int32)
    couples = (count - 1) // 2
    donor, taker = sizes[1:1 + 2 * couples:2], sizes[2:2 + 2 * couples:2]
    margin = jnp.minimum(donor - 1, bound - taker)
    shifted = jax.random.randint(jax.random.fold_in(key, 1), (couples,), 0, 1 << 20) % (margin + 1)
    sizes = sizes.at[1:1 + 2 * couples:2].set(donor - shifted).at[2:2 + 2 * couples:2].set(taker + shifted)
    return sizes[jax.random.permutation(jax.random.fold_in(key, 2), count)]


def centred(stream_key, extent, spread, most, cuts=(), kind=jnp.bfloat16):
    drawn = spread * jax.random.normal(stream_key, extent, jnp.float32)
    if cuts:
        drawn = drawn * shard_levels(stream_key, extent, cuts, -0.22, 0.18)
    return jnp.clip(drawn, -most, most).astype(kind)


def setup_inputs(seed: int = 0) -> dict:
    streams_of = jax.random.split(jax.random.key(seed), 7)
    gated_input = centred(streams_of[0], (GROUPS, FRAMES, D), 1.0, 6.0, ((0, 16), (1, 32)))
    cotangent = centred(streams_of[1], (GROUPS, FRAMES, D), 1.0, 6.0, ((0, 16), (1, 32)))
    lengths = jax.vmap(lambda own: uneven(own, UTTS, FRAMES, FRAMES // 2, 2))(jax.random.split(streams_of[2], GROUPS)).reshape((GROUPS, UTTS)).astype(jnp.int32)
    kernel = centred(streams_of[3], (KW, D), KW ** -0.5, 2.0, (), jnp.float32)
    norm_gain = jnp.clip(1.0 + 0.1 * jax.random.normal(streams_of[4], (D,), jnp.float32), 0.5, 1.5)
    out_weight = centred(streams_of[5], (D, D), D ** -0.5, 0.1875, ((0, 32),))
    return {"gated_input": gated_input, "cotangent": cotangent, "lengths": lengths, "kernel": kernel, "norm_gain": norm_gain, "out_weight": out_weight}


def utter_ids(frame_pos, lengths_row):
    bounds = jnp.cumsum(lengths_row).astype(jnp.int32)
    return lax.optimization_barrier(jnp.sum((frame_pos[:, None] >= bounds[None, :]).astype(jnp.int32), axis=1))

def normalize(conv_out, norm_gain):
    centre = conv_out - lax.optimization_barrier(jnp.mean(conv_out, axis=1, keepdims=True))
    inverse = lax.rsqrt(lax.optimization_barrier(jnp.mean(centre * centre, axis=1, keepdims=True)) + 1e-05)
    normed = centre * inverse
    return (normed, inverse, normed * norm_gain)

def back_norm(back_act, scaled, normed, inverse, norm_gain):
    logistic = jax.nn.sigmoid(scaled)
    back_scaled = back_act * (logistic * (1.0 + scaled * (1.0 - logistic)))
    hidden = back_scaled * norm_gain
    back_conv = inverse * (hidden - lax.optimization_barrier(jnp.mean(hidden, axis=1, keepdims=True)) - normed * lax.optimization_barrier(jnp.mean(hidden * normed, axis=1, keepdims=True)))
    return (back_scaled, back_conv)

def one_stream(gated_row, cot_row, lengths_row, kernel, norm_gain, out_weight):
    frames = gated_row.shape[0]
    reach = KW // 2
    frame_pos = jnp.arange(-reach, frames + reach, dtype=jnp.int32)
    ids_wide = utter_ids(frame_pos, lengths_row)
    ids_own = ids_wide[reach:reach + frames]
    padded = jnp.pad(gated_row.astype(jnp.float32), ((reach, reach), (0, 0)))
    conv_out = jnp.zeros((frames, gated_row.shape[1]), jnp.float32)
    for tap_index in range(KW):
        inside = (ids_wide[tap_index:tap_index + frames] == ids_own).astype(jnp.float32)[:, None]
        conv_out = conv_out + kernel[tap_index] * padded[tap_index:tap_index + frames] * inside
    normed, inverse, scaled = normalize(conv_out, norm_gain)
    act = (scaled * jax.nn.sigmoid(scaled)).astype(jnp.bfloat16)
    back_act = lax.dot_general(cot_row, out_weight, (((1,), (1,)), ((), ())), preferred_element_type=jnp.float32)
    back_scaled, back_conv = back_norm(back_act, scaled, normed, inverse, norm_gain)
    grad_gain = lax.optimization_barrier(jnp.sum(back_scaled * normed, axis=0))
    back_pad = jnp.pad(back_conv, ((reach, reach), (0, 0)))
    grad_rows = jnp.zeros((frames, gated_row.shape[1]), jnp.float32)
    collected = []
    for tap_index in range(KW):
        inside = (ids_wide[tap_index:tap_index + frames] == ids_own).astype(jnp.float32)[:, None]
        collected.append(lax.optimization_barrier(jnp.sum(back_conv * padded[tap_index:tap_index + frames] * inside, axis=0)))
        mirror = KW - 1 - tap_index
        inside_back = (ids_wide[mirror:mirror + frames] == ids_own).astype(jnp.float32)[:, None]
        grad_rows = grad_rows + kernel[tap_index] * back_pad[mirror:mirror + frames] * inside_back
    grad_weight = jnp.dot(act.T, cot_row, preferred_element_type=jnp.float32)
    return (grad_rows.astype(jnp.bfloat16), grad_weight, jnp.stack(collected), grad_gain)

def reference(gated_input, cotangent, lengths, kernel, norm_gain, out_weight):

    def advance(running, inputs):
        pieces = one_stream(inputs[0], inputs[1], inputs[2], kernel, norm_gain, out_weight)
        return ((running[0] + pieces[1], running[1] + pieces[2], running[2] + pieces[3]), pieces[0])
    initial = (jnp.zeros((D, D), jnp.float32), jnp.zeros((KW, D), jnp.float32), jnp.zeros((D,), jnp.float32))
    totals, grad_gated = lax.scan(advance, initial, (gated_input, cotangent, lengths))
    return (grad_gated, totals[0], totals[1], totals[2])
```

```python
import functools

import jax
import jax.numpy as jnp
from jax import lax
from jax.experimental import pallas as pl
from jax.experimental.pallas import tpu as pltpu
from jax.sharding import PartitionSpec as P

F32, BF16 = jnp.float32, jnp.bfloat16
MESH = pl.DeviceIdType.MESH
FRAMES, D, KW = 512, 1024, 9
ROWS = 32
LANES = [slice(128 * j, 128 * j + 128) for j in range(8)]


def add_up(terms):
    return functools.reduce(lambda a, b: a + b, terms)


def fold(value):
    return add_up([value[8 * q : 8 * q + 8] for q in range(value.shape[0] // 8)])


def device(x, y, z, c):
    return (lax.rem(y, 4) * 4 + x, z * 4 + lax.div(y, 4) * 2 + c)


def kernel(
    gated, cot_hbm, lengths, taps, gain, weight,
    out_rows, out_weight, out_kernel, out_gain,
    xb, cot, cot_far, halo, xw, ids, mask, kb, normed, sig, inv, act, act_far, wfull,
    back, bcw, tacc,
    ga, gd, sa1, ra1, ra2, sa2, ra3, rd1, sd1, rd2, sd2, rd3, final, gathered,
    kp, rk1, rk2, kfull,
    local, sends, recvs,
):
    dp, seq = lax.axis_index("dp"), lax.axis_index("seq")
    yl, x = lax.div(dp, 4), lax.rem(dp, 4)
    z, yh, c = lax.div(seq, 4), lax.rem(lax.div(seq, 2), 2), lax.rem(seq, 2)
    y = yh * 4 + yl
    zy = z * 2 + yh
    flip = 1 - c
    other_core = (dp, seq + 1 - 2 * c)
    before = (dp, lax.rem(seq + 31, 32))
    after = (dp, lax.rem(seq + 1, 32))
    mine = lax.div(z, 4) == c

    barrier = pltpu.get_barrier_semaphore()

    def greet(target):
        pl.semaphore_signal(barrier, inc=1, device_id=target, device_id_type=MESH)

    def column(i):
        at = lax.rem(2 * z + c + i, 16)
        return at, device(x, y, lax.div(at, 2), lax.rem(at, 2))

    def row(i):
        at = lax.rem(2 * y + c + i, 16)
        return at, device(x, lax.div(at, 2), z, lax.rem(at, 2))

    def plane(i):
        at = lax.rem(x * 8 + z + i, 32)
        return device(lax.div(at, 8), y, lax.rem(at, 8), c)

    def slabs(i):
        at = lax.rem(zy + i, 16)
        return device(x, lax.rem(at, 2) * 4 + yl, lax.div(at, 2), c)

    def streams(i):
        at = lax.rem(dp + i, 16)
        return (at, seq)

    def across_x(i):
        at = lax.rem(x + i, 4)
        return at, device(at, y, z, c)

    def across_y(i):
        at = lax.rem(y + i, 8)
        return at, device(x, at, z, c)

    def loop(low, high, step):
        def one(i, none):
            step(i)
            return none

        lax.fori_loop(low, high, one, 0)

    loop(1, 16, lambda i: greet(column(i)[1]))
    loop(1, 16, lambda i: greet(row(i)[1]))
    loop(1, 32, lambda i: greet(plane(i)))
    loop(1, 16, lambda i: greet(slabs(i)))
    loop(1, 16, lambda i: greet(streams(i)))
    greet(before)
    greet(after)

    def copy(group, source, target_ref, target):
        return pltpu.make_async_remote_copy(
            src_ref=source, dst_ref=target_ref, send_sem=sends.at[group],
            recv_sem=recvs.at[group], device_id=target, device_id_type=MESH,
        )

    def send(group, source, target_ref, target):
        copy(group, source, target_ref, target).start()

    def arrived(group, ref):
        copy(group, ref, ref, other_core).wait_recv()

    def sent(group, ref):
        copy(group, ref, ref, other_core).wait_send()

    (HALO_A, HALO_B, W_THIN, W_WIDE, W_X, W_C1, W_C2, COT, ACT, RA1, RA2, RA3, RD1, RD2, RD3,
     GATHER, K1, K2, K3, BACK_A, BACK_B) = range(21)
    ACTS = 21

    get_x = pltpu.make_async_copy(gated.at[0], xb, local.at[0])
    thin = pl.ds(pl.multiple_of(128 * x, 128), 128)
    wide = pl.ds(512, 512)
    get_thin = pltpu.make_async_copy(weight.at[:, thin], wfull.at[zy, c, :, thin], local.at[1])
    get_wide = pltpu.make_async_copy(weight.at[:, wide], wfull.at[zy, c, :, wide], local.at[3])
    get_cot = pltpu.make_async_copy(cot_hbm.at[0], cot, local.at[2])
    get_x.start()
    get_thin.start()
    get_wide.start()
    get_cot.start()

    start = seq * FRAMES
    pos = lax.broadcasted_iota(jnp.int32, (FRAMES + 16, 128), 0) + (start - 8)
    bound = jnp.int32(0)
    number = jnp.zeros((FRAMES + 16, 128), jnp.int32)
    for u in range(8):
        bound = bound + lengths[0, u]
        number = number + (pos >= bound).astype(jnp.int32)
    ids[...] = jnp.where(pos < 0, -1, number)
    for k in range(KW):
        kb[k] = jnp.broadcast_to(taps[k : k + 1, :], (8, D))
    kb[KW] = jnp.broadcast_to(gain[0:1, :], (8, D))

    def masks(i):
        r = pl.multiple_of(i * 32, 32)
        own = ids[pl.ds(r + 8, 32), :]
        for k in range(KW):
            mask[k, pl.ds(r, 32), :] = jnp.where(ids[pl.ds(r + 4 + k, 32), :] == own, 1.0, 0.0)

    loop(0, FRAMES // 32, masks)
    get_thin.wait()
    get_wide.wait()
    get_x.wait()
    pl.semaphore_wait(barrier, 15 + 15 + 31 + 15 + 15 + 2)

    send(HALO_A, xb.at[pl.ds(FRAMES - 16, 16)], halo.at[0], after)
    send(HALO_B, xb.at[pl.ds(0, 16)], halo.at[1], before)

    def send_thin(i):
        send(W_THIN, wfull.at[zy, c, :, thin], wfull.at[zy, c, :, thin], slabs(i))

    def send_wide(i):
        send(W_WIDE, wfull.at[zy, c, :, wide], wfull.at[zy, c, :, wide], slabs(i))

    loop(1, 16, send_thin)
    loop(1, 16, send_wide)
    get_cot.wait()
    send(COT, cot, cot_far, other_core)

    def widen(i):
        r = pl.multiple_of(i * 32, 32)
        value = xb[pl.ds(r, 32), :].astype(F32)
        for j in range(8):
            xw[j, pl.ds(r + 8, 32), :] = value[:, LANES[j]]

    loop(0, FRAMES // 32, widen)
    arrived(HALO_A, halo.at[0])
    arrived(HALO_B, halo.at[1])
    low, high = halo[0].astype(F32), halo[1].astype(F32)
    for j in range(8):
        xw[j, 0:8, :] = low[8:16, LANES[j]]
        xw[j, FRAMES + 8 : FRAMES + 16, :] = high[0:8, LANES[j]]

    def spread(value):
        return jnp.tile(value, (ROWS // 8, 1))

    def conv(source, r, mirrored):
        sums = []
        for j in range(8):
            terms = []
            for k in range(KW):
                lead = KW - 1 - k if mirrored else k
                terms.append(
                    spread(kb[k, :, LANES[j]])
                    * (source[j, pl.ds(r + 4 + lead, ROWS), :] * mask[lead, pl.ds(r, ROWS), :])
                )
            sums.append(add_up(terms))
        return sums

    def forward(i):
        r = pl.multiple_of(i * ROWS, ROWS)
        parts = conv(xw, r, False)
        mean = jnp.sum(add_up(parts), axis=1, keepdims=True) * (1.0 / D)
        parts = [v - mean for v in parts]
        square = jnp.sum(add_up([v * v for v in parts]), axis=1, keepdims=True) * (1.0 / D)
        scale = lax.rsqrt(square + 1e-05)
        inv[pl.ds(r, ROWS), :] = jnp.broadcast_to(scale, (ROWS, 128))
        for j in range(8):
            unit = parts[j] * scale
            normed[pl.ds(r, ROWS), LANES[j]] = unit
            scaled = unit * spread(kb[KW, :, LANES[j]])
            logistic = jax.nn.sigmoid(scaled)
            sig[pl.ds(r, ROWS), LANES[j]] = logistic
            act[j // 4, pl.ds(r, ROWS), LANES[j % 4]] = (scaled * logistic).astype(BF16)

    for q in range(4):
        loop(q * 4, q * 4 + 4, forward)
        block = pl.ds(128 * q, 128)
        send(ACTS + q, act.at[flip, block], act_far.at[block], other_core)
        if q == 2:
            arrived(W_THIN, wfull.at[pl.ds(0, 15), c, :, pl.ds(0, 128)])
            for i in (1, 3, 2):
                send(W_X, wfull.at[:, c, :, thin], wfull.at[:, c, :, thin], across_x(i)[1])

    arrived(COT, cot_far)
    for q in range(4):
        arrived(ACTS + q, act_far.at[pl.ds(128 * q, 128)])
    over_frames = (((0,), (0,)), ((), ()))
    for i in (1, 3, 2, 0):
        at, target = across_x(i)
        columns = pl.ds(pl.multiple_of(256 * at, 256), 256)
        value = lax.dot_general(
            act[c], cot[:, columns], over_frames, preferred_element_type=F32
        ) + lax.dot_general(
            act_far[...], cot_far[:, columns], over_frames, preferred_element_type=F32
        )
        gd[at] = value[:, 128:].astype(BF16).reshape(4, 2, 2, 32, 128)
        if i == 0:
            sa1[...] = value[:, :128].reshape(4, 2, 2, 4, 8, 128)
        else:
            ga[at] = value[:, :128].astype(BF16)
            send(RA1, ga.at[at], ra1.at[i - 1], target)

    def owner(t):
        zi, ci = lax.div(t, 2), lax.rem(t, 2)
        zt = 4 * c + zi
        return zi, ci, jnp.logical_and(zt == z, ci == c), device(x, y, zt, ci)

    def send_d1(t):
        zi, ci, here, target = owner(t)

        @pl.when(here)
        def _():
            rd1[z] = gd[:, zi, :, ci]

        @pl.when(jnp.logical_not(here))
        def _():
            send(RD1, gd.at[:, zi, :, ci], rd1.at[z], target)

    loop(0, 8, send_d1)

    arrived(W_WIDE, wfull.at[pl.ds(0, 15), c, :, wide])
    send(W_C1, wfull.at[:, c, :, wide], wfull.at[:, c, :, wide], other_core)
    arrived(W_X, wfull.at[pl.ds(0, 12), c, :, wide])
    send(W_C2, wfull.at[:, c, :, pl.ds(0, 512)], wfull.at[:, c, :, pl.ds(0, 512)], other_core)
    arrived(W_C1, wfull.at[:, flip, :, wide])
    arrived(W_C2, wfull.at[:, flip, :, pl.ds(0, 512)])

    def matmul(i):
        value = wfull[pl.ds(4 * i, 4)].reshape(256, D)
        back[:, pl.ds(pl.multiple_of(256 * i, 256), 256)] = lax.dot_general(
            cot[...], value, (((1,), (1,)), ((), ())), preferred_element_type=F32
        )

    loop(0, 4, matmul)

    def backward(i, sums):
        r = pl.multiple_of(i * ROWS, ROWS)
        totals, ones, twos = [], [], []
        for j in range(8):
            g = spread(kb[KW, :, LANES[j]])
            unit = normed[pl.ds(r, ROWS), LANES[j]]
            logistic = sig[pl.ds(r, ROWS), LANES[j]]
            scaled = unit * g
            value = back[pl.ds(r, ROWS), LANES[j]] * (logistic * (1.0 + scaled * (1.0 - logistic)))
            totals.append(sums[j] + fold(value * unit))
            hidden = value * g
            bcw[j, pl.ds(r + 8, ROWS), :] = hidden
            ones.append(hidden)
            twos.append(hidden * unit)
        first = jnp.sum(add_up(ones), axis=1, keepdims=True) * (1.0 / D)
        second = jnp.sum(add_up(twos), axis=1, keepdims=True) * (1.0 / D)
        scale = inv[pl.ds(r, ROWS), :]
        for j in range(8):
            unit = normed[pl.ds(r, ROWS), LANES[j]]
            bcw[j, pl.ds(r + 8, ROWS), :] = scale * (
                bcw[j, pl.ds(r + 8, ROWS), :] - first - unit * second
            )
        return tuple(totals)

    sums = lax.fori_loop(
        0, FRAMES // ROWS, backward, tuple(jnp.zeros((8, 128), F32) for _ in range(8))
    )
    send(BACK_A, bcw.at[:, pl.ds(FRAMES, 8)], bcw.at[:, pl.ds(0, 8)], after)
    send(BACK_B, bcw.at[:, pl.ds(8, 8)], bcw.at[:, pl.ds(FRAMES + 8, 8)], before)

    for k in range(KW):
        tacc[k] = jnp.zeros((8, D), F32)

    def products(i):
        r = pl.multiple_of(i * 64, 64)
        for k in range(KW):
            inside = mask[k, pl.ds(r, 64), :]
            for j in range(8):
                tacc[k, :, LANES[j]] += fold(
                    bcw[j, pl.ds(r + 8, 64), :] * (xw[j, pl.ds(r + 4 + k, 64), :] * inside)
                )

    loop(0, FRAMES // 64, products)
    for k in range(KW):
        line = jnp.sum(tacc[k], axis=0, keepdims=True)
        for j in range(8):
            kp[2 * j + k // 5, k % 5 : k % 5 + 1, :] = line[:, LANES[j]]
    for j in range(8):
        kp[2 * j + 1, 4:5, :] = jnp.sum(sums[j], axis=0, keepdims=True)

    def send_k1(i):
        at, target = row(i)
        send(K1, kp.at[at], rk1.at[i - 1], target)

    loop(1, 16, send_k1)

    arrived(RA1, ra1)
    total = sa1[...].reshape(FRAMES, 128)
    sa1[...] = (
        total + ra1[0].astype(F32) + ra1[1].astype(F32) + ra1[2].astype(F32)
    ).reshape(4, 2, 2, 4, 8, 128)

    def send_a2(i):
        at, target = across_y(i)
        send(RA2, sa1.at[:, lax.div(at, 4), :, lax.rem(at, 4)], ra2.at[i - 1], target)

    loop(1, 8, send_a2)

    def owned(group, ref):
        @pl.when(mine)
        def _():
            arrived(group, ref.at[pl.ds(0, 7)])

        @pl.when(jnp.logical_not(mine))
        def _():
            arrived(group, ref)

    owned(RD1, rd1)
    sd1[...] = add_up([rd1[i].astype(F32) for i in range(8)])
    for i in (1, 3, 2):
        at, target = across_x(i)
        send(RD2, sd1.at[at], rd2.at[i - 1], target)

    arrived(K1, rk1)
    me = x * 8 + z
    rk2[me] = add_up([kp[2 * y + c]] + [rk1[i] for i in range(15)])
    loop(1, 32, lambda i: send(K2, rk2.at[me], rk2.at[me], plane(i)))

    arrived(BACK_A, bcw.at[:, pl.ds(0, 8)])
    arrived(BACK_B, bcw.at[:, pl.ds(FRAMES + 8, 8)])

    def rows_out(i):
        r = pl.multiple_of(i * ROWS, ROWS)
        parts = conv(bcw, r, True)
        for j in range(8):
            out_rows[0, pl.ds(r, ROWS), LANES[j]] = parts[j].astype(BF16)

    loop(0, 8, rows_out)

    arrived(RA2, ra2)
    sa2[...] = add_up([sa1[:, yh, :, yl]] + [ra2[i] for i in range(7)])

    def send_a3(t):
        zi, ci, here, target = owner(t)

        @pl.when(here)
        def _():
            ra3[z] = sa2[zi, ci]

        @pl.when(jnp.logical_not(here))
        def _():
            send(RA3, sa2.at[zi, ci], ra3.at[z], target)

    loop(0, 8, send_a3)

    arrived(RD2, rd2)
    sd2[...] = add_up([sd1[x], rd2[0], rd2[1], rd2[2]]).reshape(2, 4, 8, 128)

    def send_d3(i):
        at, target = across_y(i)
        send(RD3, sd2.at[lax.div(at, 4), lax.rem(at, 4)], rd3.at[i - 1], target)

    loop(1, 8, send_d3)

    loop(8, 16, rows_out)

    arrived(K2, rk2.at[pl.ds(0, 31)])
    own = 2 * y + c
    kfull[own] = add_up([rk2[i] for i in range(32)])
    loop(1, 16, lambda i: send(K3, kfull.at[own], kfull.at[own], row(i)[1]))

    owned(RA3, ra3)
    final[:, 0:128] = add_up([ra3[i] for i in range(8)])
    arrived(RD3, rd3)
    final[:, 128:256] = add_up([sd2[yh, yl]] + [rd3[i] for i in range(7)])
    gathered[dp] = final[...]
    loop(1, 16, lambda i: send(GATHER, final, gathered.at[dp], streams(i)))

    arrived(K3, kfull.at[pl.ds(0, 15)])
    for j in range(8):
        out_kernel[0:5, LANES[j]] = kfull[2 * j]
        out_kernel[5:9, LANES[j]] = kfull[2 * j + 1, 0:4]
        out_gain[0:1, LANES[j]] = kfull[2 * j + 1, 4:5]
    arrived(GATHER, gathered.at[pl.ds(0, 15)])
    for a in range(4):
        for b in range(4):
            out_weight[8 * a : 8 * a + 8, 256 * b : 256 * b + 256] = gathered[4 * a + b]

    sent(HALO_A, halo.at[0])
    sent(HALO_B, halo.at[1])
    sent(W_THIN, wfull.at[pl.ds(0, 15), c, :, pl.ds(0, 128)])
    sent(W_WIDE, wfull.at[pl.ds(0, 15), c, :, wide])
    sent(W_X, wfull.at[pl.ds(0, 12), c, :, wide])
    sent(W_C1, wfull.at[:, c, :, wide])
    sent(W_C2, wfull.at[:, c, :, wide])
    sent(COT, cot)
    for q in range(4):
        sent(ACTS + q, act_far.at[pl.ds(128 * q, 128)])
    sent(RA1, ra1)
    sent(RA2, ra2)

    @pl.when(mine)
    def _():
        sent(RA3, ra3.at[pl.ds(0, 7)])
        sent(RD1, rd1.at[pl.ds(0, 7)])

    @pl.when(jnp.logical_not(mine))
    def _():
        sent(RA3, ra3)
        sent(RD1, rd1)

    sent(RD2, rd2)
    sent(RD3, rd3)
    sent(GATHER, gathered.at[pl.ds(0, 15)])
    sent(K1, rk1)
    sent(K2, rk2.at[pl.ds(0, 31)])
    sent(K3, kfull.at[pl.ds(0, 15)])
    sent(BACK_A, bcw.at[:, pl.ds(0, 8)])
    sent(BACK_B, bcw.at[:, pl.ds(0, 8)])


def body(gated, cotangent, lengths, taps, gain, weight):
    v = pltpu.VMEM
    vmem, hbm = pl.BlockSpec(memory_space=v), pl.BlockSpec(memory_space=pl.ANY)
    rows, dweight, dkernel, dgain = pl.pallas_call(
        kernel,
        out_shape=(
            jax.ShapeDtypeStruct((1, FRAMES, D), BF16),
            jax.ShapeDtypeStruct((32, D), F32),
            jax.ShapeDtypeStruct((KW, D), F32),
            jax.ShapeDtypeStruct((1, D), F32),
        ),
        in_specs=[hbm, hbm, pl.BlockSpec(memory_space=pltpu.SMEM), vmem, vmem, hbm],
        out_specs=(vmem, vmem, vmem, vmem),
        scratch_shapes=[
            v((FRAMES, D), BF16),
            v((FRAMES, D), BF16),
            v((FRAMES, D), BF16),
            v((2, 16, D), BF16),
            v((8, FRAMES + 16, 128), F32),
            v((FRAMES + 16, 128), jnp.int32),
            v((KW, FRAMES, 128), F32),
            v((KW + 1, 8, D), F32),
            v((FRAMES, D), F32),
            v((FRAMES, D), F32),
            v((FRAMES, 128), F32),
            v((2, FRAMES, 512), BF16),
            v((FRAMES, 512), BF16),
            v((16, 2, 32, D), BF16),
            v((FRAMES, D), F32),
            v((8, FRAMES + 16, 128), F32),
            v((KW, 8, D), F32),
            v((4, FRAMES, 128), BF16),
            v((4, 4, 2, 2, 32, 128), BF16),
            v((4, 2, 2, 4, 8, 128), F32),
            v((3, FRAMES, 128), BF16),
            v((7, 4, 2, 8, 128), F32),
            v((4, 2, 8, 128), F32),
            v((8, 8, 128), F32),
            v((8, 4, 2, 32, 128), BF16),
            v((4, 2, 32, 128), F32),
            v((3, 2, 32, 128), F32),
            v((2, 4, 8, 128), F32),
            v((7, 8, 128), F32),
            v((8, 256), F32),
            v((16, 8, 256), F32),
            v((16, 5, 128), F32),
            v((15, 5, 128), F32),
            v((32, 5, 128), F32),
            v((16, 5, 128), F32),
            pltpu.SemaphoreType.DMA((4,)),
            pltpu.SemaphoreType.DMA((25,)),
            pltpu.SemaphoreType.DMA((25,)),
        ],
        compiler_params=pltpu.CompilerParams(
            collective_id=1, has_side_effects=True, vmem_limit_bytes=48 << 20
        ),
    )(gated, cotangent, lengths, taps, gain.reshape(1, D), weight)
    return rows, dweight, dkernel, dgain.reshape(D)


def solution(mesh):
    return jax.shard_map(
        body,
        mesh=mesh,
        in_specs=(
            P("dp", "seq", None),
            P("dp", "seq", None),
            P("dp", None),
            P(),
            P(),
            P("seq", None),
        ),
        out_specs=(P("dp", "seq", None), P("seq", None), P(), P()),
        check_vma=False,
    )
```

```python
import functools

import jax
import jax.numpy as jnp
from jax import lax
from jax.experimental import pallas as pl
from jax.experimental.pallas import tpu as pltpu
from jax.sharding import PartitionSpec as P

F32, BF16 = jnp.float32, jnp.bfloat16
MESH = pl.DeviceIdType.MESH
FRAMES, D, KW = 512, 1024, 9
ROWS = 32
LANES = [slice(128 * j, 128 * j + 128) for j in range(8)]


def add_up(terms):
    return functools.reduce(lambda a, b: a + b, terms)


def fold(value):
    return add_up([value[8 * q : 8 * q + 8] for q in range(value.shape[0] // 8)])


def device(x, y, z, c):
    return ((y & 3) * 4 + x, z * 4 + (y >> 2) * 2 + c)


def kernel(
    gated, cot_hbm, lengths_hbm, taps_hbm, gain_hbm, weight,
    out_rows, out_weight, out_kernel, out_gain,
    xb, cot, cot_far, halo, relay, xw, ids, mask, kb, normed, sig, inv, act, act_far, wfull,
    back, bcw, tacc,
    ga, gd, sa1, ra1, ra2, sa2, ra3, rd1, sd1, rd2, sd2, rd3, final, gathered,
    kp, rk1, rk2, kfull, lengths, taps, gain, rows,
    local, sends, recvs,
):
    dp, seq = lax.axis_index("dp"), lax.axis_index("seq")
    yl, x = dp >> 2, dp & 3
    z, yh, c = seq >> 2, (seq >> 1) & 1, seq & 1
    y = yh * 4 + yl
    flip = 1 - c
    other_core = (dp, seq + 1 - 2 * c)
    before = (dp, ((seq + 31) & 31))
    after = (dp, ((seq + 1) & 31))
    mine = (z >> 2) == c

    barrier = pltpu.get_barrier_semaphore()

    def greet(target):
        pl.semaphore_signal(barrier, inc=1, device_id=target, device_id_type=MESH)

    def row(i):
        at = (2 * y + c + i) & 15
        return at, device(x, at >> 1, z, at & 1)

    def plane(i):
        at = (x * 8 + z + i) & 31
        return device(at >> 3, y, at & 7, c)

    def streams(i):
        at = (dp + i) & 15
        return (at, seq)

    def across_x(i):
        at = (x + i) & 3
        return at, device(at, y, z, c)

    def across_y(i):
        at = (y + i) & 7
        return at, device(x, at, z, c)

    def across_z(i):
        return device(x, y, ((z + i) & 7), c)

    mirror = device(x, 7 - y, z, c)

    def loop(low, high, step):
        def one(i, none):
            step(i)
            return none

        lax.fori_loop(low, high, one, 0)

    for i in (4, 3, 5, 2, 6, 1, 7):
        greet(across_z(i))
        greet(across_y(i)[1])
    for i in (2, 1, 3):
        greet(across_x(i)[1])
    greet(other_core)

    def copy(group, source, target_ref, target):
        return pltpu.make_async_remote_copy(
            src_ref=source, dst_ref=target_ref, send_sem=sends.at[group],
            recv_sem=recvs.at[group], device_id=target, device_id_type=MESH,
        )

    def send(group, source, target_ref, target):
        started.add(group)
        pending.add(group)
        copy(group, source, target_ref, target).start()

    def arrived(group):
        whole = size_of[group]
        if group in SPLIT:
            owned(group, whole, "wait_recv")
        else:
            copy(group, whole, whole, other_core).wait_recv()
        pending.discard(group)

    def sent(group):
        whole = size_of[group]
        if group == RELAY:
            pl.when(crossing)(lambda: copy(group, whole, whole, other_core).wait_send())
        elif group in SPLIT:
            owned(group, whole, "wait_send")
        else:
            copy(group, whole, whole, other_core).wait_send()

    def owned(group, whole, wait):
        @pl.when(mine)
        def _():
            part = whole.at[pl.ds(0, 7)]
            getattr(copy(group, part, part, other_core), wait)()

        @pl.when(jnp.logical_not(mine))
        def _():
            getattr(copy(group, whole, whole, other_core), wait)()

    (HALO_NEAR, HALO_FAR, RELAY, W_MIRROR, W_Z1, W_Z2, W_Z3, W_S1, W_S2, W_XOWN, W_XSIB, W_Y, W_C1, W_C2, W_C3,
     COT, RA1, RA2, RA3, RD1, RD2, RD3, GATHER, K1, K2, K3, BACK_A, BACK_B) = range(28)
    ACTS = 28
    SPLIT = (RA3, RD1)
    started, pending = set(), set()
    seven = wfull.at[pl.ds(0, 7), 0, 0]
    size_of = {
        HALO_NEAR: halo.at[0], HALO_FAR: halo.at[0], RELAY: relay,
        W_MIRROR: wfull.at[0, 0, 0, :, pl.ds(0, 384)],
        W_Z1: seven.at[:, :, pl.ds(0, 128)], W_S1: seven.at[:, :, pl.ds(0, 128)],
        W_Z2: seven.at[:, :, pl.ds(0, 256)], W_S2: seven.at[:, :, pl.ds(0, 256)],
        W_Z3: seven.at[:, pl.ds(0, 16), pl.ds(0, 128)],
        W_XOWN: wfull.at[:, 0, 0, :, pl.ds(0, 384)], W_XSIB: wfull.at[:, 0, 0, :, pl.ds(0, 384)],
        W_Y: wfull.at[:, 0, 0, pl.ds(0, 16), pl.ds(0, 896)],
        W_C1: wfull.at[:, 0, 0, :, pl.ds(0, 512)], W_C2: wfull.at[:, 0, 0, :, pl.ds(0, 512)],
        W_C3: wfull.at[:, 0, :, :, pl.ds(0, 512)],
        COT: cot_far,
        RA1: ra1, RA2: ra2, RA3: ra3, RD1: rd1, RD2: rd2, RD3: rd3,
        GATHER: gathered.at[pl.ds(0, 15)],
        K1: rk1, K2: rk2.at[pl.ds(0, 31)], K3: kfull.at[pl.ds(0, 15)],
        BACK_A: bcw.at[:, pl.ds(0, 8)], BACK_B: bcw.at[:, pl.ds(0, 8)],
    }
    for q in range(4):
        size_of[ACTS + q] = act_far.at[pl.ds(128 * q, 128)]

    get_x = pltpu.make_async_copy(gated.at[0], xb, local.at[0])
    thin = pl.ds(pl.multiple_of(128 * x, 128), 128)
    direct = pl.ds(512, 256)
    corner = (
        pl.ds(pl.multiple_of(16 * (yl >> 1), 16), 16),
        pl.ds(pl.multiple_of(768 + 128 * (yl & 1), 128), 128),
    )
    get_w = [
        pltpu.make_async_copy(weight.at[:, thin], wfull.at[z, yh, c, :, thin], local.at[1]),
        pltpu.make_async_copy(weight.at[:, direct], wfull.at[z, yh, c, :, direct], local.at[3]),
        pltpu.make_async_copy(weight.at[corner], wfull.at[(z, yh, c) + corner], local.at[7]),
    ]
    get_cot = pltpu.make_async_copy(cot_hbm.at[0], cot, local.at[2])
    small = [
        pltpu.make_async_copy(source, target, local.at[4 + i])
        for i, (source, target) in enumerate(
            ((lengths_hbm, lengths), (taps_hbm, taps), (gain_hbm, gain))
        )
    ]
    for get in get_w + [get_x] + small + [get_cot]:
        get.start()

    for get in get_w:
        get.wait()
    pl.semaphore_wait(barrier, 1 + 3 + 7 + 7)

    def same(group, part, target):
        send(group, part, part, target)

    own_thin, own_direct = wfull.at[z, yh, c, :, thin], wfull.at[z, yh, c, :, direct]
    own_corner = wfull.at[(z, yh, c) + corner]
    same(W_MIRROR, own_thin, mirror)
    same(W_MIRROR, own_direct, mirror)
    for i in (4, 3, 5, 2, 6, 1, 7):
        same(W_Z1, own_thin, across_z(i))
    get_x.wait()
    last, first = xb.at[pl.ds(FRAMES - 16, 16)], xb.at[pl.ds(0, 16)]
    crossing = yh == c
    opposite = device(x, (y + 4) & 7, z, 1 - c)

    @pl.when(c == 1)
    def _():
        send(HALO_NEAR, first, halo.at[1], other_core)

    @pl.when(c == 0)
    def _():
        send(HALO_NEAR, last, halo.at[0], other_core)

    @pl.when(jnp.logical_and(crossing, c == 1))
    def _():
        send(RELAY, last, relay, across_z(1))

    @pl.when(jnp.logical_and(crossing, c == 0))
    def _():
        send(RELAY, first, relay, across_z(7))

    loop(1, 8, lambda i: same(W_Z3, own_corner, across_z(i)))
    loop(1, 8, lambda i: same(W_Z2, own_direct, across_z(i)))
    get_cot.wait()
    send(COT, cot, cot_far, other_core)
    for get in small:
        get.wait()

    start = seq * FRAMES
    pos = lax.broadcasted_iota(jnp.int32, (FRAMES + 16, 128), 0) + (start - 8)
    bound = jnp.int32(0)
    number = jnp.zeros((FRAMES + 16, 128), jnp.int32)
    for u in range(8):
        bound = bound + lengths[0, u]
        number = number + (pos >= bound).astype(jnp.int32)
    ids[...] = jnp.where(pos < 0, -1, number)
    for k in range(KW):
        kb[k] = jnp.broadcast_to(taps[k : k + 1, :], (8, D))
    kb[KW] = jnp.broadcast_to(gain[0:1, :], (8, D))

    def masks(i):
        r = pl.multiple_of(i * 32, 32)
        own = ids[pl.ds(r + 8, 32), :]
        for k in range(KW):
            mask[k, pl.ds(r, 32), :] = jnp.where(ids[pl.ds(r + 4 + k, 32), :] == own, 1.0, 0.0)

    loop(0, FRAMES // 32, masks)

    def widen(i):
        r = pl.multiple_of(i * 32, 32)
        value = xb[pl.ds(r, 32), :].astype(F32)
        for j in range(8):
            xw[j, pl.ds(r + 8, 32), :] = value[:, LANES[j]]

    loop(0, FRAMES // 32, widen)

    def spread(value):
        return jnp.tile(value, (ROWS // 8, 1))

    def conv(source, r, mirrored):
        sums = []
        for j in range(8):
            terms = []
            for k in range(KW):
                lead = KW - 1 - k if mirrored else k
                terms.append(
                    spread(kb[k, :, LANES[j]])
                    * (source[j, pl.ds(r + 4 + lead, ROWS), :] * mask[lead, pl.ds(r, ROWS), :])
                )
            sums.append(add_up(terms))
        return sums

    def forward(i):
        r = pl.multiple_of(i * ROWS, ROWS)
        parts = conv(xw, r, False)
        mean = jnp.sum(add_up(parts), axis=1, keepdims=True) * (1.0 / D)
        parts = [v - mean for v in parts]
        square = jnp.sum(add_up([v * v for v in parts]), axis=1, keepdims=True) * (1.0 / D)
        scale = lax.rsqrt(square + 1e-05)
        inv[pl.ds(r, ROWS), :] = jnp.broadcast_to(scale, (ROWS, 128))
        for j in range(8):
            unit = parts[j] * scale
            normed[pl.ds(r, ROWS), LANES[j]] = unit
            scaled = unit * spread(kb[KW, :, LANES[j]])
            logistic = jax.nn.sigmoid(scaled)
            sig[pl.ds(r, ROWS), LANES[j]] = logistic
            act[j // 4, pl.ds(r, ROWS), LANES[j % 4]] = (scaled * logistic).astype(BF16)

    def send_act(q):
        block = pl.ds(128 * q, 128)
        send(ACTS + q, act.at[flip, block], act_far.at[block], other_core)

    loop(4, 8, forward)
    send_act(1)
    arrived(COT)

    @pl.when(crossing)
    def _():
        arrived(RELAY)

        @pl.when(c == 1)
        def _():
            send(HALO_FAR, relay, halo.at[0], opposite)

        @pl.when(c == 0)
        def _():
            send(HALO_FAR, relay, halo.at[1], opposite)

    @pl.when(jnp.logical_and(jnp.logical_not(crossing), c == 1))
    def _():
        send(HALO_FAR, last, halo.at[0], opposite)

    @pl.when(jnp.logical_and(jnp.logical_not(crossing), c == 0))
    def _():
        send(HALO_FAR, first, halo.at[1], opposite)

    loop(8, 12, forward)
    send_act(2)
    arrived(W_MIRROR)
    sib_thin, sib_direct = wfull.at[z, 1 - yh, c, :, thin], wfull.at[z, 1 - yh, c, :, direct]
    loop(1, 8, lambda i: same(W_S1, sib_thin, across_z(i)))
    loop(1, 8, lambda i: same(W_S2, sib_direct, across_z(i)))
    loop(1, 4, forward)
    arrived(W_Z1)
    for i in (1, 3, 2):
        same(W_XOWN, wfull.at[:, yh, c, :, thin], across_x(i)[1])
    arrived(W_Z3)
    own_corners = wfull.at[(slice(None), yh, c) + corner]
    loop(1, 8, lambda i: same(W_Y, own_corners, across_y(i)[1]))
    loop(12, 15, forward)
    arrived(HALO_NEAR)
    arrived(HALO_FAR)
    low, high = halo[0].astype(F32), halo[1].astype(F32)
    for j in range(8):
        xw[j, 0:8, :] = low[8:16, LANES[j]]
        xw[j, FRAMES + 8 : FRAMES + 16, :] = high[0:8, LANES[j]]
    forward(0)
    send_act(0)
    forward(15)
    send_act(3)

    for q in range(4):
        arrived(ACTS + q)
    over_frames = (((0,), (0,)), ((), ()))
    for i in (1, 3, 2, 0):
        at, target = across_x(i)
        columns = pl.ds(pl.multiple_of(256 * at, 256), 256)
        value = lax.dot_general(
            act[c], cot[:, columns], over_frames, preferred_element_type=F32
        ) + lax.dot_general(
            act_far[...], cot_far[:, columns], over_frames, preferred_element_type=F32
        )
        gd[at] = value[:, 128:].astype(BF16).reshape(4, 2, 2, 32, 128)
        if i == 0:
            sa1[...] = value[:, :128].reshape(4, 2, 2, 4, 8, 128)
        else:
            ga[at] = value[:, :128].astype(BF16)
        if i == 3:
            arrived(W_S1)
            for k in (1, 3, 2):
                same(W_XSIB, wfull.at[:, 1 - yh, c, :, thin], across_x(k)[1])

    def owner(t):
        zi, ci = t >> 1, t & 1
        zt = 4 * c + zi
        return zi, ci, jnp.logical_and(zt == z, ci == c), device(x, y, zt, ci)

    def send_d1(t):
        zi, ci, here, target = owner(t)

        @pl.when(here)
        def _():
            rd1[z] = gd[:, zi, :, ci]

        @pl.when(jnp.logical_not(here))
        def _():
            send(RD1, gd.at[:, zi, :, ci], rd1.at[z], target)

    for i in (1, 3, 2):
        at, target = across_x(i)
        send(RA1, ga.at[at], ra1.at[i - 1], target)
    loop(0, 8, send_d1)

    first_half, second_half = pl.ds(0, 512), pl.ds(512, 512)
    arrived(W_XOWN)
    same(W_C1, wfull.at[:, yh, c, :, first_half], other_core)
    arrived(W_Z2)
    arrived(W_S2)
    arrived(W_Y)
    same(W_C3, wfull.at[:, :, c, :, second_half], other_core)
    arrived(W_XSIB)
    same(W_C2, wfull.at[:, 1 - yh, c, :, first_half], other_core)
    arrived(W_C3)
    arrived(W_C1)
    arrived(W_C2)

    def matmul(i):
        value = wfull[pl.ds(2 * i, 2)].reshape(256, D)
        back[:, pl.ds(pl.multiple_of(256 * i, 256), 256)] = lax.dot_general(
            cot[...], value, (((1,), (1,)), ((), ())), preferred_element_type=F32
        )

    loop(0, 4, matmul)

    def backward(i, sums):
        r = pl.multiple_of(i * ROWS, ROWS)
        totals, ones, twos = [], [], []
        for j in range(8):
            g = spread(kb[KW, :, LANES[j]])
            unit = normed[pl.ds(r, ROWS), LANES[j]]
            logistic = sig[pl.ds(r, ROWS), LANES[j]]
            scaled = unit * g
            value = back[pl.ds(r, ROWS), LANES[j]] * (logistic * (1.0 + scaled * (1.0 - logistic)))
            totals.append(sums[j] + fold(value * unit))
            hidden = value * g
            bcw[j, pl.ds(r + 8, ROWS), :] = hidden
            ones.append(hidden)
            twos.append(hidden * unit)
        first = jnp.sum(add_up(ones), axis=1, keepdims=True) * (1.0 / D)
        second = jnp.sum(add_up(twos), axis=1, keepdims=True) * (1.0 / D)
        scale = inv[pl.ds(r, ROWS), :]
        for j in range(8):
            unit = normed[pl.ds(r, ROWS), LANES[j]]
            bcw[j, pl.ds(r + 8, ROWS), :] = scale * (
                bcw[j, pl.ds(r + 8, ROWS), :] - first - unit * second
            )
        return tuple(totals)

    sums = lax.fori_loop(
        0, FRAMES // ROWS, backward, tuple(jnp.zeros((8, 128), F32) for _ in range(8))
    )
    send(BACK_A, bcw.at[:, pl.ds(FRAMES, 8)], bcw.at[:, pl.ds(0, 8)], after)
    send(BACK_B, bcw.at[:, pl.ds(8, 8)], bcw.at[:, pl.ds(FRAMES + 8, 8)], before)

    for k in range(KW):
        tacc[k] = jnp.zeros((8, D), F32)

    def products(i):
        r = pl.multiple_of(i * 64, 64)
        for k in range(KW):
            inside = mask[k, pl.ds(r, 64), :]
            for j in range(8):
                tacc[k, :, LANES[j]] += fold(
                    bcw[j, pl.ds(r + 8, 64), :] * (xw[j, pl.ds(r + 4 + k, 64), :] * inside)
                )

    loop(0, FRAMES // 64, products)
    for k in range(KW):
        line = jnp.sum(tacc[k], axis=0, keepdims=True)
        for j in range(8):
            kp[2 * j + k // 5, k % 5 : k % 5 + 1, :] = line[:, LANES[j]]
    for j in range(8):
        kp[2 * j + 1, 4:5, :] = jnp.sum(sums[j], axis=0, keepdims=True)

    def send_k1(i):
        at, target = row(i)
        send(K1, kp.at[at], rk1.at[i - 1], target)

    loop(1, 16, send_k1)

    arrived(RA1)
    total = sa1[...].reshape(FRAMES, 128)
    sa1[...] = (
        total + ra1[0].astype(F32) + ra1[1].astype(F32) + ra1[2].astype(F32)
    ).reshape(4, 2, 2, 4, 8, 128)

    def send_a2(i):
        at, target = across_y(i)
        send(RA2, sa1.at[:, at >> 2, :, at & 3], ra2.at[i - 1], target)

    loop(1, 8, send_a2)

    arrived(RD1)
    sd1[...] = add_up([rd1[i].astype(F32) for i in range(8)])
    for i in (1, 3, 2):
        at, target = across_x(i)
        send(RD2, sd1.at[at], rd2.at[i - 1], target)

    arrived(K1)
    me = x * 8 + z
    rk2[me] = add_up([kp[2 * y + c]] + [rk1[i] for i in range(15)])
    loop(1, 32, lambda i: send(K2, rk2.at[me], rk2.at[me], plane(i)))

    arrived(BACK_A)
    arrived(BACK_B)

    put_rows = [
        pltpu.make_async_copy(rows.at[half], out_rows.at[0, half], local.at[8 + i])
        for i, half in enumerate((pl.ds(0, 256), pl.ds(256, 256)))
    ]

    def rows_out(i):
        r = pl.multiple_of(i * ROWS, ROWS)
        parts = conv(bcw, r, True)
        for j in range(8):
            rows[pl.ds(r, ROWS), LANES[j]] = parts[j].astype(BF16)

    loop(0, 8, rows_out)
    put_rows[0].start()

    arrived(RA2)
    sa2[...] = add_up([sa1[:, yh, :, yl]] + [ra2[i] for i in range(7)])

    def send_a3(t):
        zi, ci, here, target = owner(t)

        @pl.when(here)
        def _():
            ra3[z] = sa2[zi, ci]

        @pl.when(jnp.logical_not(here))
        def _():
            send(RA3, sa2.at[zi, ci], ra3.at[z], target)

    loop(0, 8, send_a3)

    arrived(RD2)
    sd2[...] = add_up([sd1[x], rd2[0], rd2[1], rd2[2]]).reshape(2, 4, 8, 128)

    def send_d3(i):
        at, target = across_y(i)
        send(RD3, sd2.at[at >> 2, at & 3], rd3.at[i - 1], target)

    loop(1, 8, send_d3)

    loop(8, 16, rows_out)
    put_rows[1].start()

    arrived(K2)
    own = 2 * y + c
    kfull[own] = add_up([rk2[i] for i in range(32)])
    loop(1, 16, lambda i: send(K3, kfull.at[own], kfull.at[own], row(i)[1]))

    arrived(RA3)
    final[:, 0:128] = add_up([ra3[i] for i in range(8)])
    arrived(RD3)
    final[:, 128:256] = add_up([sd2[yh, yl]] + [rd3[i] for i in range(7)])
    gathered[dp] = final[...]
    loop(1, 16, lambda i: send(GATHER, final, gathered.at[dp], streams(i)))

    arrived(K3)
    for j in range(8):
        out_kernel[0:5, LANES[j]] = kfull[2 * j]
        out_kernel[5:9, LANES[j]] = kfull[2 * j + 1, 0:4]
        out_gain[0:1, LANES[j]] = kfull[2 * j + 1, 4:5]
    arrived(GATHER)
    for a in range(4):
        for b in range(4):
            out_weight[8 * a : 8 * a + 8, 256 * b : 256 * b + 256] = gathered[4 * a + b]

    put_rows[0].wait()
    put_rows[1].wait()
    for group in sorted(started):
        sent(group)


def hand_over(*refs):
    source, target, held, sems = refs[0:4], refs[4:8], refs[8:12], refs[12]
    parts = [(0, (0, pl.ds(128 * q, 128))) for q in range(4)] + [(i, ...) for i in (1, 2, 3)]
    into, out = [], []
    for i, (k, at) in enumerate(parts):
        into.append(pltpu.make_async_copy(source[k].at[at], held[k].at[at], sems.at[0, i]))
        out.append(pltpu.make_async_copy(held[k].at[at], target[k].at[at], sems.at[1, i]))
    for one in into:
        one.start()
    for first, second in zip(into, out):
        first.wait()
        second.start()
    for one in out:
        one.wait()


def body(gated, cotangent, lengths, taps, gain, weight):
    v = pltpu.VMEM
    vmem, hbm = pl.BlockSpec(memory_space=v), pl.BlockSpec(memory_space=pl.ANY)
    rows, dweight, dkernel, dgain = pl.pallas_call(
        kernel,
        out_shape=(
            jax.ShapeDtypeStruct((1, FRAMES, D), BF16),
            jax.ShapeDtypeStruct((32, D), F32),
            jax.ShapeDtypeStruct((KW, D), F32),
            jax.ShapeDtypeStruct((1, D), F32),
        ),
        in_specs=[hbm] * 6,
        out_specs=(hbm, vmem, vmem, vmem),
        scratch_shapes=[
            v((FRAMES, D), BF16),
            v((FRAMES, D), BF16),
            v((FRAMES, D), BF16),
            v((2, 16, D), BF16),
            v((16, D), BF16),
            v((8, FRAMES + 16, 128), F32),
            v((FRAMES + 16, 128), jnp.int32),
            v((KW, FRAMES, 128), F32),
            v((KW + 1, 8, D), F32),
            v((FRAMES, D), F32),
            v((FRAMES, D), F32),
            v((FRAMES, 128), F32),
            v((2, FRAMES, 512), BF16),
            v((FRAMES, 512), BF16),
            v((8, 2, 2, 32, D), BF16),
            v((FRAMES, D), F32),
            v((8, FRAMES + 16, 128), F32),
            v((KW, 8, D), F32),
            v((4, FRAMES, 128), BF16),
            v((4, 4, 2, 2, 32, 128), BF16),
            v((4, 2, 2, 4, 8, 128), F32),
            v((3, FRAMES, 128), BF16),
            v((7, 4, 2, 8, 128), F32),
            v((4, 2, 8, 128), F32),
            v((8, 8, 128), F32),
            v((8, 4, 2, 32, 128), BF16),
            v((4, 2, 32, 128), F32),
            v((3, 2, 32, 128), F32),
            v((2, 4, 8, 128), F32),
            v((7, 8, 128), F32),
            v((8, 256), F32),
            v((16, 8, 256), F32),
            v((16, 5, 128), F32),
            v((15, 5, 128), F32),
            v((32, 5, 128), F32),
            v((16, 5, 128), F32),
            pltpu.SMEM((1, 8), jnp.int32),
            v((KW, D), F32),
            v((1, D), F32),
            v((FRAMES, D), BF16),
            pltpu.SemaphoreType.DMA((10,)),
            pltpu.SemaphoreType.DMA((32,)),
            pltpu.SemaphoreType.DMA((32,)),
        ],
        compiler_params=pltpu.CompilerParams(
            collective_id=1, has_side_effects=True, vmem_limit_bytes=60 << 20
        ),
    )(gated, cotangent, lengths, taps, gain.reshape(1, D), weight)
    results = (rows, dweight, dkernel, dgain)
    rows, dweight, dkernel, dgain = pl.pallas_call(
        hand_over,
        out_shape=tuple(jax.ShapeDtypeStruct(r.shape, r.dtype) for r in results),
        in_specs=[hbm] * 4,
        out_specs=(hbm,) * 4,
        scratch_shapes=[v(r.shape, r.dtype) for r in results] + [pltpu.SemaphoreType.DMA((2, 7))],
        compiler_params=pltpu.CompilerParams(vmem_limit_bytes=60 << 20),
    )(*results)
    return rows, dweight, dkernel, dgain.reshape(D)


def solution(mesh):
    return jax.shard_map(
        body,
        mesh=mesh,
        in_specs=(
            P("dp", "seq", None),
            P("dp", "seq", None),
            P("dp", None),
            P(),
            P(),
            P("seq", None),
        ),
        out_specs=(P("dp", "seq", None), P("seq", None), P(), P()),
        check_vma=False,
    )
```

```python
import functools

import jax
import jax.numpy as jnp
from jax import lax
from jax.experimental import pallas as pl
from jax.experimental.pallas import tpu as pltpu
from jax.sharding import PartitionSpec as P

F32, BF16 = jnp.float32, jnp.bfloat16
MESH = pl.DeviceIdType.MESH
FRAMES, D, KW = 512, 1024, 9
ROWS = 32
LANES = [slice(128 * j, 128 * j + 128) for j in range(8)]


def add_up(terms):
    return functools.reduce(lambda a, b: a + b, terms)


def fold(value):
    return add_up([value[8 * q : 8 * q + 8] for q in range(value.shape[0] // 8)])


def device(x, y, z, c):
    return ((y & 3) * 4 + x, z * 4 + (y >> 2) * 2 + c)


def kernel(
    gated, cot_hbm, lengths_hbm, taps_hbm, gain_hbm, weight,
    out_rows, out_weight, out_kernel, out_gain,
    xb, cot, cot_far, halo, relay, xw, ids, mask, kb, normed, sig, inv, act, act_far, wfull,
    back, bcw, tacc,
    ga, gd, sa1, sb1, ra1, ra2, sa2, ra3, rd1, sd1, rd2, sd2, rd3, final, gathered,
    kp, rk1, rk2, kfull, lengths, taps, gain,
    local, sends, recvs,
):
    dp, seq = lax.axis_index("dp"), lax.axis_index("seq")
    yl, x = dp >> 2, dp & 3
    z, yh, c = seq >> 2, (seq >> 1) & 1, seq & 1
    y = yh * 4 + yl
    flip = 1 - c
    other_core = (dp, seq + 1 - 2 * c)
    before = (dp, ((seq + 31) & 31))
    after = (dp, ((seq + 1) & 31))
    mine = (z >> 2) == c

    barrier = pltpu.get_barrier_semaphore()

    def greet(target):
        pl.semaphore_signal(barrier, inc=1, device_id=target, device_id_type=MESH)

    def row(i):
        at = (2 * y + c + i) & 15
        return at, device(x, at >> 1, z, at & 1)

    def plane(i):
        at = (x * 8 + z + i) & 31
        return device(at >> 3, y, at & 7, c)

    def streams(i):
        at = (dp + i) & 15
        return (at, seq)

    def across_x(i):
        at = (x + i) & 3
        return at, device(at, y, z, c)

    def across_y(i):
        at = (y + i) & 7
        return at, device(x, at, z, c)

    def across_z(i):
        return device(x, y, ((z + i) & 7), c)

    mirror = device(x, 7 - y, z, c)

    def loop(low, high, step):
        def one(i, none):
            step(i)
            return none

        lax.fori_loop(low, high, one, 0)

    for i in (4, 3, 5, 2, 6, 1, 7):
        greet(across_z(i))
        greet(across_y(i)[1])
    for i in (2, 1, 3):
        greet(across_x(i)[1])
    greet(other_core)

    def copy(group, source, target_ref, target):
        return pltpu.make_async_remote_copy(
            src_ref=source, dst_ref=target_ref, send_sem=sends.at[group],
            recv_sem=recvs.at[group], device_id=target, device_id_type=MESH,
        )

    def send(group, source, target_ref, target):
        started.add(group)
        pending.add(group)
        copy(group, source, target_ref, target).start()

    def arrived(group):
        whole = size_of[group]
        if group in SPLIT:
            owned(group, whole, "wait_recv")
        else:
            copy(group, whole, whole, other_core).wait_recv()
        pending.discard(group)

    def sent(group):
        whole = size_of[group]
        if group == RELAY:
            pl.when(crossing)(lambda: copy(group, whole, whole, other_core).wait_send())
        elif group in SPLIT:
            owned(group, whole, "wait_send")
        else:
            copy(group, whole, whole, other_core).wait_send()

    def owned(group, whole, wait):
        @pl.when(mine)
        def _():
            part = whole.at[pl.ds(0, 7)]
            getattr(copy(group, part, part, other_core), wait)()

        @pl.when(jnp.logical_not(mine))
        def _():
            getattr(copy(group, whole, whole, other_core), wait)()

    (HALO_NEAR, HALO_FAR, RELAY, W_MIRROR, W_Z1, W_Z2, W_Z3, W_S1, W_S2, W_XOWN, W_XSIB, W_Y, W_C1, W_C2, W_C3,
     COT, RA1, RA2, RA3, RD1, RD2, RD3, GATHER, K1, K2, K3, BACK_A, BACK_B) = range(28)
    ACTS = 28
    SPLIT = (RA3, RD1)
    started, pending = set(), set()
    seven = wfull.at[pl.ds(0, 7), 0, 0]
    size_of = {
        HALO_NEAR: halo.at[0], HALO_FAR: halo.at[0], RELAY: relay,
        W_MIRROR: wfull.at[0, 0, 0, :, pl.ds(0, 384)],
        W_Z1: seven.at[:, :, pl.ds(0, 128)], W_S1: seven.at[:, :, pl.ds(0, 128)],
        W_Z2: seven.at[:, :, pl.ds(0, 256)], W_S2: seven.at[:, :, pl.ds(0, 256)],
        W_Z3: seven.at[:, pl.ds(0, 16), pl.ds(0, 128)],
        W_XOWN: wfull.at[:, 0, 0, :, pl.ds(0, 384)], W_XSIB: wfull.at[:, 0, 0, :, pl.ds(0, 384)],
        W_Y: wfull.at[:, 0, 0, pl.ds(0, 16), pl.ds(0, 896)],
        W_C1: wfull.at[:, 0, 0, :, pl.ds(0, 512)], W_C2: wfull.at[:, 0, 0, :, pl.ds(0, 512)],
        W_C3: wfull.at[:, 0, :, :, pl.ds(0, 512)],
        COT: cot_far,
        RA1: ra1, RA2: ra2, RA3: ra3, RD1: rd1, RD2: rd2, RD3: rd3,
        GATHER: gathered.at[pl.ds(0, 15)],
        K1: rk1, K2: rk2.at[pl.ds(0, 31)], K3: kfull.at[pl.ds(0, 15)],
        BACK_A: bcw.at[:, pl.ds(0, 8)], BACK_B: bcw.at[:, pl.ds(0, 8)],
    }
    for q in range(4):
        size_of[ACTS + q] = act_far.at[pl.ds(128 * q, 128)]

    get_x = pltpu.make_async_copy(gated.at[0], xb, local.at[0])
    thin = pl.ds(pl.multiple_of(128 * x, 128), 128)
    direct = pl.ds(512, 256)
    corner = (
        pl.ds(pl.multiple_of(16 * (yl >> 1), 16), 16),
        pl.ds(pl.multiple_of(768 + 128 * (yl & 1), 128), 128),
    )
    get_w = [
        pltpu.make_async_copy(weight.at[:, thin], wfull.at[z, yh, c, :, thin], local.at[1]),
        pltpu.make_async_copy(weight.at[:, direct], wfull.at[z, yh, c, :, direct], local.at[3]),
        pltpu.make_async_copy(weight.at[corner], wfull.at[(z, yh, c) + corner], local.at[7]),
    ]
    get_cot = pltpu.make_async_copy(cot_hbm.at[0], cot, local.at[2])
    small = [
        pltpu.make_async_copy(source, target, local.at[4 + i])
        for i, (source, target) in enumerate(
            ((lengths_hbm, lengths), (taps_hbm, taps), (gain_hbm, gain))
        )
    ]
    for get in get_w + [get_x] + small + [get_cot]:
        get.start()

    for get in get_w:
        get.wait()
    pl.semaphore_wait(barrier, 1 + 3 + 7 + 7)

    def same(group, part, target):
        send(group, part, part, target)

    own_thin, own_direct = wfull.at[z, yh, c, :, thin], wfull.at[z, yh, c, :, direct]
    own_corner = wfull.at[(z, yh, c) + corner]
    same(W_MIRROR, own_thin, mirror)
    same(W_MIRROR, own_direct, mirror)
    for i in (4, 3, 5, 2, 6, 1, 7):
        same(W_Z1, own_thin, across_z(i))
    get_x.wait()
    last, first = xb.at[pl.ds(FRAMES - 16, 16)], xb.at[pl.ds(0, 16)]
    crossing = yh == c
    opposite = device(x, (y + 4) & 7, z, 1 - c)

    @pl.when(c == 1)
    def _():
        send(HALO_NEAR, first, halo.at[1], other_core)

    @pl.when(c == 0)
    def _():
        send(HALO_NEAR, last, halo.at[0], other_core)

    @pl.when(jnp.logical_and(crossing, c == 1))
    def _():
        send(RELAY, last, relay, across_z(1))

    @pl.when(jnp.logical_and(crossing, c == 0))
    def _():
        send(RELAY, first, relay, across_z(7))

    loop(1, 8, lambda i: same(W_Z3, own_corner, across_z(i)))
    loop(1, 8, lambda i: same(W_Z2, own_direct, across_z(i)))
    get_cot.wait()
    send(COT, cot, cot_far, other_core)
    for get in small:
        get.wait()

    start = seq * FRAMES
    pos = lax.broadcasted_iota(jnp.int32, (FRAMES + 16, 128), 0) + (start - 8)
    bound = jnp.int32(0)
    number = jnp.zeros((FRAMES + 16, 128), jnp.int32)
    for u in range(8):
        bound = bound + lengths[0, u]
        number = number + (pos >= bound).astype(jnp.int32)
    ids[...] = jnp.where(pos < 0, -1, number)
    for k in range(KW):
        kb[k] = jnp.broadcast_to(taps[k : k + 1, :], (8, D))
    kb[KW] = jnp.broadcast_to(gain[0:1, :], (8, D))

    def masks(i):
        r = pl.multiple_of(i * 32, 32)
        own = ids[pl.ds(r + 8, 32), :]
        for k in range(KW):
            mask[k, pl.ds(r, 32), :] = jnp.where(ids[pl.ds(r + 4 + k, 32), :] == own, 1.0, 0.0)

    loop(0, FRAMES // 32, masks)

    def widen(i):
        r = pl.multiple_of(i * 32, 32)
        value = xb[pl.ds(r, 32), :].astype(F32)
        for j in range(8):
            xw[j, pl.ds(r + 8, 32), :] = value[:, LANES[j]]

    loop(0, FRAMES // 32, widen)

    def spread(value):
        return jnp.tile(value, (ROWS // 8, 1))

    def conv(source, r, mirrored):
        sums = []
        for j in range(8):
            terms = []
            for k in range(KW):
                lead = KW - 1 - k if mirrored else k
                terms.append(
                    spread(kb[k, :, LANES[j]])
                    * (source[j, pl.ds(r + 4 + lead, ROWS), :] * mask[lead, pl.ds(r, ROWS), :])
                )
            sums.append(add_up(terms))
        return sums

    def forward(i):
        r = pl.multiple_of(i * ROWS, ROWS)
        parts = conv(xw, r, False)
        mean = jnp.sum(add_up(parts), axis=1, keepdims=True) * (1.0 / D)
        parts = [v - mean for v in parts]
        square = jnp.sum(add_up([v * v for v in parts]), axis=1, keepdims=True) * (1.0 / D)
        scale = lax.rsqrt(square + 1e-05)
        inv[pl.ds(r, ROWS), :] = jnp.broadcast_to(scale, (ROWS, 128))
        for j in range(8):
            unit = parts[j] * scale
            normed[pl.ds(r, ROWS), LANES[j]] = unit
            scaled = unit * spread(kb[KW, :, LANES[j]])
            logistic = jax.nn.sigmoid(scaled)
            sig[pl.ds(r, ROWS), LANES[j]] = logistic
            act[j // 4, pl.ds(r, ROWS), LANES[j % 4]] = (scaled * logistic).astype(BF16)

    def send_act(q):
        block = pl.ds(128 * q, 128)
        send(ACTS + q, act.at[flip, block], act_far.at[block], other_core)

    sib_thin, sib_direct = wfull.at[z, 1 - yh, c, :, thin], wfull.at[z, 1 - yh, c, :, direct]

    def step(t):
        @pl.when(t == 2)
        def _():
            arrived(COT)

            @pl.when(crossing)
            def _():
                arrived(RELAY)

                @pl.when(c == 1)
                def _():
                    send(HALO_FAR, relay, halo.at[0], opposite)

                @pl.when(c == 0)
                def _():
                    send(HALO_FAR, relay, halo.at[1], opposite)

            @pl.when(jnp.logical_and(jnp.logical_not(crossing), c == 1))
            def _():
                send(HALO_FAR, last, halo.at[0], opposite)

            @pl.when(jnp.logical_and(jnp.logical_not(crossing), c == 0))
            def _():
                send(HALO_FAR, first, halo.at[1], opposite)

        @pl.when(t == 4)
        def _():
            arrived(W_MIRROR)
            loop(1, 8, lambda i: same(W_S1, sib_thin, across_z(i)))
            loop(1, 8, lambda i: same(W_S2, sib_direct, across_z(i)))

        @pl.when(t == 7)
        def _():
            arrived(W_Z1)
            for i in (1, 3, 2):
                same(W_XOWN, wfull.at[:, yh, c, :, thin], across_x(i)[1])
            arrived(W_Z3)
            own_corners = wfull.at[(slice(None), yh, c) + corner]
            loop(1, 8, lambda i: same(W_Y, own_corners, across_y(i)[1]))

        @pl.when(t == 14)
        def _():
            arrived(HALO_NEAR)
            arrived(HALO_FAR)
            low, high = halo[0].astype(F32), halo[1].astype(F32)
            for j in range(8):
                xw[j, 0:8, :] = low[8:16, LANES[j]]
                xw[j, FRAMES + 8 : FRAMES + 16, :] = high[0:8, LANES[j]]

        forward((t + 1) & 15)
        for q, last_step in ((1, 6), (2, 10), (3, 14), (0, 15)):
            pl.when(t == last_step)(functools.partial(send_act, q))

    loop(0, 16, step)

    for q in range(4):
        arrived(ACTS + q)
    over_frames = (((0,), (0,)), ((), ()))

    def product(t):
        at = (x + t + 1) & 3
        columns = pl.ds(pl.multiple_of(256 * at, 256), 256)
        value = lax.dot_general(
            act[c], cot[:, columns], over_frames, preferred_element_type=F32
        ) + lax.dot_general(
            act_far[...], cot_far[:, columns], over_frames, preferred_element_type=F32
        )
        gd[at] = value[:, 128:].astype(BF16).reshape(4, 2, 2, 32, 128)
        ga[at] = value[:, :128].astype(BF16)
        sa1[...] = value[:, :128]

        @pl.when(t == 0)
        def _():
            arrived(W_S1)
            for k in (1, 3, 2):
                same(W_XSIB, wfull.at[:, 1 - yh, c, :, thin], across_x(k)[1])

    loop(0, 4, product)
    def owner(t):
        zi, ci = t >> 1, t & 1
        zt = 4 * c + zi
        return zi, ci, jnp.logical_and(zt == z, ci == c), device(x, y, zt, ci)

    def send_d1(t):
        zi, ci, here, target = owner(t)

        @pl.when(here)
        def _():
            rd1[z] = gd[:, zi, :, ci]

        @pl.when(jnp.logical_not(here))
        def _():
            send(RD1, gd.at[:, zi, :, ci], rd1.at[z], target)

    for i in (1, 3, 2):
        at, target = across_x(i)
        send(RA1, ga.at[at], ra1.at[i - 1], target)
    loop(0, 8, send_d1)

    first_half, second_half = pl.ds(0, 512), pl.ds(512, 512)
    arrived(W_XOWN)
    same(W_C1, wfull.at[:, yh, c, :, first_half], other_core)
    arrived(W_Z2)
    arrived(W_S2)
    arrived(W_Y)
    same(W_C3, wfull.at[:, :, c, :, second_half], other_core)
    arrived(W_XSIB)
    same(W_C2, wfull.at[:, 1 - yh, c, :, first_half], other_core)
    arrived(W_C3)
    arrived(W_C1)
    arrived(W_C2)

    def matmul(i):
        value = wfull[pl.ds(2 * i, 2)].reshape(256, D)
        back[:, pl.ds(pl.multiple_of(256 * i, 256), 256)] = lax.dot_general(
            cot[...], value, (((1,), (1,)), ((), ())), preferred_element_type=F32
        )

    loop(0, 4, matmul)

    def backward(i, sums):
        r = pl.multiple_of(i * ROWS, ROWS)
        totals, ones, twos = [], [], []
        for j in range(8):
            g = spread(kb[KW, :, LANES[j]])
            unit = normed[pl.ds(r, ROWS), LANES[j]]
            logistic = sig[pl.ds(r, ROWS), LANES[j]]
            scaled = unit * g
            value = back[pl.ds(r, ROWS), LANES[j]] * (logistic * (1.0 + scaled * (1.0 - logistic)))
            totals.append(sums[j] + fold(value * unit))
            hidden = value * g
            bcw[j, pl.ds(r + 8, ROWS), :] = hidden
            ones.append(hidden)
            twos.append(hidden * unit)
        first = jnp.sum(add_up(ones), axis=1, keepdims=True) * (1.0 / D)
        second = jnp.sum(add_up(twos), axis=1, keepdims=True) * (1.0 / D)
        scale = inv[pl.ds(r, ROWS), :]
        for j in range(8):
            unit = normed[pl.ds(r, ROWS), LANES[j]]
            bcw[j, pl.ds(r + 8, ROWS), :] = scale * (
                bcw[j, pl.ds(r + 8, ROWS), :] - first - unit * second
            )
        return tuple(totals)

    sums = lax.fori_loop(
        0, FRAMES // ROWS, backward, tuple(jnp.zeros((8, 128), F32) for _ in range(8))
    )
    send(BACK_A, bcw.at[:, pl.ds(FRAMES, 8)], bcw.at[:, pl.ds(0, 8)], after)
    send(BACK_B, bcw.at[:, pl.ds(8, 8)], bcw.at[:, pl.ds(FRAMES + 8, 8)], before)

    for k in range(KW):
        tacc[k] = jnp.zeros((8, D), F32)

    def products(i):
        r = pl.multiple_of(i * 64, 64)
        for k in range(KW):
            inside = mask[k, pl.ds(r, 64), :]
            for j in range(8):
                tacc[k, :, LANES[j]] += fold(
                    bcw[j, pl.ds(r + 8, 64), :] * (xw[j, pl.ds(r + 4 + k, 64), :] * inside)
                )

    loop(0, FRAMES // 64, products)
    for k in range(KW):
        line = jnp.sum(tacc[k], axis=0, keepdims=True)
        for j in range(8):
            kp[2 * j + k // 5, k % 5 : k % 5 + 1, :] = line[:, LANES[j]]
    for j in range(8):
        kp[2 * j + 1, 4:5, :] = jnp.sum(sums[j], axis=0, keepdims=True)

    def send_k1(i):
        at, target = row(i)
        send(K1, kp.at[at], rk1.at[i - 1], target)

    loop(1, 16, send_k1)

    arrived(RA1)
    total = add_up([sa1[...]] + [ra1[i].astype(F32) for i in range(3)])
    total = jnp.swapaxes(total.reshape(4, 2, 2, 4, 8, 128), 2, 3).reshape(4, 2, 4, 16, 128)
    sa1[...] = total.reshape(FRAMES, 128)
    sb1[...] = total.astype(BF16)

    def send_a2(i):
        at, target = across_y(i)
        send(RA2, sb1.at[:, at >> 2, at & 3], ra2.at[i - 1], target)

    loop(1, 8, send_a2)

    arrived(RD1)
    sd1[...] = add_up([rd1[i].astype(F32) for i in range(8)])
    for i in (1, 3, 2):
        at, target = across_x(i)
        send(RD2, sd1.at[at], rd2.at[i - 1], target)

    arrived(K1)
    me = x * 8 + z
    rk2[me] = add_up([kp[2 * y + c]] + [rk1[i] for i in range(15)])
    loop(1, 32, lambda i: send(K2, rk2.at[me], rk2.at[me], plane(i)))

    arrived(BACK_A)
    arrived(BACK_B)

    def rows_out(i):
        r = pl.multiple_of(i * ROWS, ROWS)
        parts = conv(bcw, r, True)
        for j in range(8):
            out_rows[0, pl.ds(r, ROWS), LANES[j]] = parts[j].astype(BF16)

    def send_a3(t):
        zi, ci, here, target = owner(t)

        @pl.when(here)
        def _():
            ra3[z] = sa2[zi, ci]

        @pl.when(jnp.logical_not(here))
        def _():
            send(RA3, sa2.at[zi, ci], ra3.at[z], target)

    def send_d3(i):
        at, target = across_y(i)
        send(RD3, sd2.at[at >> 2, at & 3], rd3.at[i - 1], target)

    def result(t):
        @pl.when(t == 8)
        def _():
            arrived(RA2)
            for i in range(4):
                own_rows = pl.ds(pl.multiple_of(128 * i + 64 * yh + 16 * yl, 16), 16)
                pieces = [sa1[own_rows, :]] + [ra2[k, i].astype(F32) for k in range(7)]
                sa2[i] = add_up(pieces).reshape(2, 8, 128)

            loop(0, 8, send_a3)
            arrived(RD2)
            sd2[...] = add_up([sd1[x], rd2[0], rd2[1], rd2[2]]).reshape(2, 4, 8, 128)

            loop(1, 8, send_d3)

        rows_out(t)

    loop(0, 16, result)

    arrived(K2)
    own = 2 * y + c
    kfull[own] = add_up([rk2[i] for i in range(32)])
    loop(1, 16, lambda i: send(K3, kfull.at[own], kfull.at[own], row(i)[1]))

    arrived(RA3)
    final[:, 0:128] = add_up([ra3[i] for i in range(8)])
    arrived(RD3)
    final[:, 128:256] = add_up([sd2[yh, yl]] + [rd3[i] for i in range(7)])
    gathered[dp] = final[...]
    loop(1, 16, lambda i: send(GATHER, final, gathered.at[dp], streams(i)))

    arrived(K3)
    for j in range(8):
        out_kernel[0:5, LANES[j]] = kfull[2 * j]
        out_kernel[5:9, LANES[j]] = kfull[2 * j + 1, 0:4]
        out_gain[0:1, LANES[j]] = kfull[2 * j + 1, 4:5]
    arrived(GATHER)
    for a in range(4):
        for b in range(4):
            out_weight[8 * a : 8 * a + 8, 256 * b : 256 * b + 256] = gathered[4 * a + b]

    for group in sorted(started):
        sent(group)


def hand_over(*refs):
    copies = [pltpu.make_async_copy(refs[i], refs[4 + i], refs[8].at[i]) for i in range(4)]
    for one in copies:
        one.start()
    for one in copies:
        one.wait()


def body(gated, cotangent, lengths, taps, gain, weight):
    v = pltpu.VMEM
    vmem, hbm = pl.BlockSpec(memory_space=v), pl.BlockSpec(memory_space=pltpu.HBM)
    rows, dweight, dkernel, dgain = pl.pallas_call(
        kernel,
        out_shape=(
            v((1, FRAMES, D), BF16),
            v((32, D), F32),
            v((KW, D), F32),
            v((1, D), F32),
        ),
        in_specs=[hbm] * 6,
        out_specs=(vmem,) * 4,
        scratch_shapes=[
            v((FRAMES, D), BF16),
            v((FRAMES, D), BF16),
            v((FRAMES, D), BF16),
            v((2, 16, D), BF16),
            v((16, D), BF16),
            v((8, FRAMES + 16, 128), F32),
            v((FRAMES + 16, 128), jnp.int32),
            v((KW, FRAMES, 128), F32),
            v((KW + 1, 8, D), F32),
            v((FRAMES, D), F32),
            v((FRAMES, D), F32),
            v((FRAMES, 128), F32),
            v((2, FRAMES, 512), BF16),
            v((FRAMES, 512), BF16),
            v((8, 2, 2, 32, D), BF16),
            v((FRAMES, D), F32),
            v((8, FRAMES + 16, 128), F32),
            v((KW, 8, D), F32),
            v((4, FRAMES, 128), BF16),
            v((4, 4, 2, 2, 32, 128), BF16),
            v((FRAMES, 128), F32),
            v((4, 2, 4, 16, 128), BF16),
            v((3, FRAMES, 128), BF16),
            v((7, 4, 16, 128), BF16),
            v((4, 2, 8, 128), F32),
            v((8, 8, 128), F32),
            v((8, 4, 2, 32, 128), BF16),
            v((4, 2, 32, 128), F32),
            v((3, 2, 32, 128), F32),
            v((2, 4, 8, 128), F32),
            v((7, 8, 128), F32),
            v((8, 256), F32),
            v((16, 8, 256), F32),
            v((16, 5, 128), F32),
            v((15, 5, 128), F32),
            v((32, 5, 128), F32),
            v((16, 5, 128), F32),
            pltpu.SMEM((1, 8), jnp.int32),
            v((KW, D), F32),
            v((1, D), F32),
            pltpu.SemaphoreType.DMA((8,)),
            pltpu.SemaphoreType.DMA((32,)),
            pltpu.SemaphoreType.DMA((32,)),
        ],
        compiler_params=pltpu.CompilerParams(
            collective_id=1, has_side_effects=True, vmem_limit_bytes=60 << 20
        ),
    )(gated, cotangent, lengths, taps, gain.reshape(1, D), weight)
    results = (rows, dweight, dkernel, dgain)
    rows, dweight, dkernel, dgain = pl.pallas_call(
        hand_over,
        out_shape=tuple(jax.ShapeDtypeStruct(r.shape, r.dtype) for r in results),
        in_specs=[vmem] * 4,
        out_specs=(hbm,) * 4,
        scratch_shapes=[pltpu.SemaphoreType.DMA((4,))],
        compiler_params=pltpu.CompilerParams(vmem_limit_bytes=32 << 20),
    )(*results)
    return rows, dweight, dkernel, dgain.reshape(D)


def solution(mesh):
    return jax.shard_map(
        body,
        mesh=mesh,
        in_specs=(
            P("dp", "seq", None),
            P("dp", "seq", None),
            P("dp", None),
            P(),
            P(),
            P("seq", None),
        ),
        out_specs=(P("dp", "seq", None), P("seq", None), P(), P()),
        check_vma=False,
    )
```

```python
import functools

import jax
import jax.numpy as jnp
from jax import lax
from jax.experimental import pallas as pl
from jax.experimental.pallas import tpu as pltpu
from jax.sharding import PartitionSpec as P

F32, BF16 = jnp.float32, jnp.bfloat16
MESH = pl.DeviceIdType.MESH
FRAMES, D, KW = 512, 1024, 9
ROWS = 32
LANES = [slice(128 * j, 128 * j + 128) for j in range(8)]


def add_up(terms):
    return functools.reduce(lambda a, b: a + b, terms)


def fold(value):
    return add_up([value[8 * q : 8 * q + 8] for q in range(value.shape[0] // 8)])


def device(x, y, z, c):
    return ((y & 3) * 4 + x, z * 4 + (y >> 2) * 2 + c)


def kernel(
    gated, cot_hbm, lengths_hbm, taps_hbm, gain_hbm, weight,
    out_rows, out_weight, out_kernel, out_gain,
    xb, cot, cot_far, halo, relay, xw, ids, mask, kb, normed, slope, inv, act, act_far, wfull,
    back, bcw, tacc,
    ga, gd, sa1, sb1, ra1, ra2, sa2, ra3, rd1, sd1, rd2, sd2, rd3, final, gathered,
    kp, rk1, rk2, kfull, lengths, taps, gain,
    local, sends, recvs,
):
    dp, seq = lax.axis_index("dp"), lax.axis_index("seq")
    yl, x = dp >> 2, dp & 3
    z, yh, c = seq >> 2, (seq >> 1) & 1, seq & 1
    y = yh * 4 + yl
    flip = 1 - c
    other_core = (dp, seq + 1 - 2 * c)
    before = (dp, ((seq + 31) & 31))
    after = (dp, ((seq + 1) & 31))
    mine = (z >> 2) == c

    barrier = pltpu.get_barrier_semaphore()

    def greet(target):
        pl.semaphore_signal(barrier, inc=1, device_id=target, device_id_type=MESH)

    def row(i):
        at = (2 * y + c + i) & 15
        return at, device(x, at >> 1, z, at & 1)

    def plane(i):
        at = (x * 8 + z + i) & 31
        return device(at >> 3, y, at & 7, c)

    def streams(i):
        at = (dp + i) & 15
        return (at, seq)

    def across_x(i):
        at = (x + i) & 3
        return at, device(at, y, z, c)

    def across_y(i):
        at = (y + i) & 7
        return at, device(x, at, z, c)

    def across_z(i):
        return device(x, y, ((z + i) & 7), c)

    mirror = device(x, 7 - y, z, c)

    def loop(low, high, step):
        def one(i, none):
            step(i)
            return none

        lax.fori_loop(low, high, one, 0)

    for i in (4, 3, 5, 2, 6, 1, 7):
        greet(across_z(i))
        greet(across_y(i)[1])
    for i in (2, 1, 3):
        greet(across_x(i)[1])
    greet(other_core)

    def copy(group, source, target_ref, target):
        return pltpu.make_async_remote_copy(
            src_ref=source, dst_ref=target_ref, send_sem=sends.at[group],
            recv_sem=recvs.at[group], device_id=target, device_id_type=MESH,
        )

    def send(group, source, target_ref, target):
        started.add(group)
        pending.add(group)
        copy(group, source, target_ref, target).start()

    def arrived(group):
        whole = size_of[group]
        if group in SPLIT:
            owned(group, whole, "wait_recv")
        else:
            copy(group, whole, whole, other_core).wait_recv()
        pending.discard(group)

    def sent(group):
        whole = size_of[group]
        if group == RELAY:
            pl.when(crossing)(lambda: copy(group, whole, whole, other_core).wait_send())
        elif group in SPLIT:
            owned(group, whole, "wait_send")
        else:
            copy(group, whole, whole, other_core).wait_send()

    def owned(group, whole, wait):
        @pl.when(mine)
        def _():
            part = whole.at[pl.ds(0, 7)]
            getattr(copy(group, part, part, other_core), wait)()

        @pl.when(jnp.logical_not(mine))
        def _():
            getattr(copy(group, whole, whole, other_core), wait)()

    (HALO_NEAR, HALO_FAR, RELAY, W_MIRROR, W_Z1, W_Z2, W_Z3, W_S1, W_S2, W_XOWN, W_XSIB, W_Y, W_C1, W_C2, W_C3,
     COT, RA1, RA2, RA3, RD1, RD2, RD3, GATHER, K1, K2, K3, BACK_A, BACK_B) = range(28)
    ACTS = 28
    SPLIT = (RA3, RD1)
    started, pending = set(), set()
    seven = wfull.at[pl.ds(0, 7), 0, 0]
    size_of = {
        HALO_NEAR: halo.at[0], HALO_FAR: halo.at[0], RELAY: relay,
        W_MIRROR: wfull.at[0, 0, 0, :, pl.ds(0, 384)],
        W_Z1: seven.at[:, :, pl.ds(0, 128)], W_S1: seven.at[:, :, pl.ds(0, 128)],
        W_Z2: seven.at[:, :, pl.ds(0, 256)], W_S2: seven.at[:, :, pl.ds(0, 256)],
        W_Z3: seven.at[:, pl.ds(0, 16), pl.ds(0, 128)],
        W_XOWN: wfull.at[:, 0, 0, :, pl.ds(0, 384)], W_XSIB: wfull.at[:, 0, 0, :, pl.ds(0, 384)],
        W_Y: wfull.at[:, 0, 0, pl.ds(0, 16), pl.ds(0, 896)],
        W_C1: wfull.at[:, 0, 0, :, pl.ds(0, 512)], W_C2: wfull.at[:, 0, 0, :, pl.ds(0, 512)],
        W_C3: wfull.at[:, 0, :, :, pl.ds(0, 512)],
        COT: cot_far,
        RA1: ra1, RA2: ra2, RA3: ra3, RD1: rd1, RD2: rd2, RD3: rd3,
        GATHER: gathered.at[pl.ds(0, 15)],
        K1: rk1, K2: rk2.at[pl.ds(0, 31)], K3: kfull.at[pl.ds(0, 15)],
        BACK_A: bcw.at[:, pl.ds(0, 8)], BACK_B: bcw.at[:, pl.ds(0, 8)],
    }
    for q in range(4):
        size_of[ACTS + q] = act_far.at[pl.ds(128 * q, 128)]

    get_x = pltpu.make_async_copy(gated.at[0], xb, local.at[0])
    thin = pl.ds(pl.multiple_of(128 * x, 128), 128)
    direct = pl.ds(512, 256)
    corner = (
        pl.ds(pl.multiple_of(16 * (yl >> 1), 16), 16),
        pl.ds(pl.multiple_of(768 + 128 * (yl & 1), 128), 128),
    )
    get_w = [
        pltpu.make_async_copy(weight.at[:, thin], wfull.at[z, yh, c, :, thin], local.at[1]),
        pltpu.make_async_copy(weight.at[:, direct], wfull.at[z, yh, c, :, direct], local.at[3]),
        pltpu.make_async_copy(weight.at[corner], wfull.at[(z, yh, c) + corner], local.at[7]),
    ]
    get_cot = pltpu.make_async_copy(cot_hbm.at[0], cot, local.at[2])
    small = [
        pltpu.make_async_copy(source, target, local.at[4 + i])
        for i, (source, target) in enumerate(
            ((lengths_hbm, lengths), (taps_hbm, taps), (gain_hbm, gain))
        )
    ]
    for get in get_w + [get_x] + small + [get_cot]:
        get.start()

    for get in get_w:
        get.wait()
    pl.semaphore_wait(barrier, 1 + 3 + 7 + 7)

    def same(group, part, target):
        send(group, part, part, target)

    own_thin, own_direct = wfull.at[z, yh, c, :, thin], wfull.at[z, yh, c, :, direct]
    own_corner = wfull.at[(z, yh, c) + corner]
    same(W_MIRROR, own_thin, mirror)
    same(W_MIRROR, own_direct, mirror)
    for i in (4, 3, 5, 2, 6, 1, 7):
        same(W_Z1, own_thin, across_z(i))
    get_x.wait()
    last, first = xb.at[pl.ds(FRAMES - 16, 16)], xb.at[pl.ds(0, 16)]
    crossing = yh == c
    opposite = device(x, (y + 4) & 7, z, 1 - c)

    @pl.when(c == 1)
    def _():
        send(HALO_NEAR, first, halo.at[1], other_core)

    @pl.when(c == 0)
    def _():
        send(HALO_NEAR, last, halo.at[0], other_core)

    @pl.when(jnp.logical_and(crossing, c == 1))
    def _():
        send(RELAY, last, relay, across_z(1))

    @pl.when(jnp.logical_and(crossing, c == 0))
    def _():
        send(RELAY, first, relay, across_z(7))

    loop(1, 8, lambda i: same(W_Z3, own_corner, across_z(i)))
    loop(1, 8, lambda i: same(W_Z2, own_direct, across_z(i)))
    get_cot.wait()
    send(COT, cot, cot_far, other_core)
    for get in small:
        get.wait()

    start = seq * FRAMES
    pos = lax.broadcasted_iota(jnp.int32, (FRAMES + 16, 128), 0) + (start - 8)
    bound = jnp.int32(0)
    number = jnp.zeros((FRAMES + 16, 128), jnp.int32)
    for u in range(8):
        bound = bound + lengths[0, u]
        number = number + (pos >= bound).astype(jnp.int32)
    ids[...] = jnp.where(pos < 0, -1, number)
    for k in range(KW):
        kb[k] = jnp.broadcast_to(taps[k : k + 1, :], (8, D))
    kb[KW] = jnp.broadcast_to(gain[0:1, :], (8, D))

    def masks(i):
        r = pl.multiple_of(i * 32, 32)
        own = ids[pl.ds(r + 8, 32), :]
        for k in range(KW):
            mask[k, pl.ds(r, 32), :] = jnp.where(ids[pl.ds(r + 4 + k, 32), :] == own, 1.0, 0.0)

    loop(0, FRAMES // 32, masks)

    def widen(i):
        r = pl.multiple_of(i * 32, 32)
        value = xb[pl.ds(r, 32), :].astype(F32)
        for j in range(8):
            xw[j, pl.ds(r + 8, 32), :] = value[:, LANES[j]]

    loop(0, FRAMES // 32, widen)

    def spread(value):
        return jnp.tile(value, (ROWS // 8, 1))

    def conv(source, r, mirrored):
        sums = []
        for j in range(8):
            terms = []
            for k in range(KW):
                lead = KW - 1 - k if mirrored else k
                terms.append(
                    spread(kb[k, :, LANES[j]])
                    * (source[j, pl.ds(r + 4 + lead, ROWS), :] * mask[lead, pl.ds(r, ROWS), :])
                )
            sums.append(add_up(terms))
        return sums

    def forward(i):
        r = pl.multiple_of(i * ROWS, ROWS)
        parts = conv(xw, r, False)
        mean = jnp.sum(add_up(parts), axis=1, keepdims=True) * (1.0 / D)
        parts = [v - mean for v in parts]
        square = jnp.sum(add_up([v * v for v in parts]), axis=1, keepdims=True) * (1.0 / D)
        scale = lax.rsqrt(square + 1e-05)
        inv[pl.ds(r, ROWS), :] = jnp.broadcast_to(scale, (ROWS, 128))
        for j in range(8):
            unit = parts[j] * scale
            normed[pl.ds(r, ROWS), LANES[j]] = unit
            scaled = unit * spread(kb[KW, :, LANES[j]])
            logistic = jax.nn.sigmoid(scaled)
            slope[pl.ds(r, ROWS), LANES[j]] = logistic * (1.0 + scaled * (1.0 - logistic))
            act[j // 4, pl.ds(r, ROWS), LANES[j % 4]] = (scaled * logistic).astype(BF16)

    def send_act(q):
        block = pl.ds(128 * q, 128)
        send(ACTS + q, act.at[flip, block], act_far.at[block], other_core)

    sib_thin, sib_direct = wfull.at[z, 1 - yh, c, :, thin], wfull.at[z, 1 - yh, c, :, direct]

    def step(t):
        @pl.when(t == 2)
        def _():
            arrived(COT)

            @pl.when(crossing)
            def _():
                arrived(RELAY)

                @pl.when(c == 1)
                def _():
                    send(HALO_FAR, relay, halo.at[0], opposite)

                @pl.when(c == 0)
                def _():
                    send(HALO_FAR, relay, halo.at[1], opposite)

            @pl.when(jnp.logical_and(jnp.logical_not(crossing), c == 1))
            def _():
                send(HALO_FAR, last, halo.at[0], opposite)

            @pl.when(jnp.logical_and(jnp.logical_not(crossing), c == 0))
            def _():
                send(HALO_FAR, first, halo.at[1], opposite)

        @pl.when(t == 4)
        def _():
            arrived(W_MIRROR)
            loop(1, 8, lambda i: same(W_S1, sib_thin, across_z(i)))
            loop(1, 8, lambda i: same(W_S2, sib_direct, across_z(i)))

        @pl.when(t == 7)
        def _():
            arrived(W_Z1)
            for i in (1, 3, 2):
                same(W_XOWN, wfull.at[:, yh, c, :, thin], across_x(i)[1])
            arrived(W_Z3)
            own_corners = wfull.at[(slice(None), yh, c) + corner]
            loop(1, 8, lambda i: same(W_Y, own_corners, across_y(i)[1]))

        @pl.when(t == 14)
        def _():
            arrived(HALO_NEAR)
            arrived(HALO_FAR)
            low, high = halo[0].astype(F32), halo[1].astype(F32)
            for j in range(8):
                xw[j, 0:8, :] = low[8:16, LANES[j]]
                xw[j, FRAMES + 8 : FRAMES + 16, :] = high[0:8, LANES[j]]

        forward((t + 1) & 15)
        for q, last_step in ((1, 6), (2, 10), (3, 14), (0, 15)):
            pl.when(t == last_step)(functools.partial(send_act, q))

    loop(0, 16, step)

    for q in range(4):
        arrived(ACTS + q)
    over_frames = (((0,), (0,)), ((), ()))

    def product(t):
        at = (x + t + 1) & 3
        columns = pl.ds(pl.multiple_of(256 * at, 256), 256)
        value = lax.dot_general(
            act[c], cot[:, columns], over_frames, preferred_element_type=F32
        ) + lax.dot_general(
            act_far[...], cot_far[:, columns], over_frames, preferred_element_type=F32
        )
        gd[at] = value[:, 128:].astype(BF16).reshape(4, 2, 2, 32, 128)
        ga[at] = value[:, :128].astype(BF16)
        sa1[...] = value[:, :128]

        @pl.when(t == 0)
        def _():
            arrived(W_S1)
            for k in (1, 3, 2):
                same(W_XSIB, wfull.at[:, 1 - yh, c, :, thin], across_x(k)[1])

    loop(0, 4, product)
    def owner(t):
        zi, ci = t >> 1, t & 1
        zt = 4 * c + zi
        return zi, ci, jnp.logical_and(zt == z, ci == c), device(x, y, zt, ci)

    def send_d1(t):
        zi, ci, here, target = owner(t)

        @pl.when(here)
        def _():
            rd1[z] = gd[:, zi, :, ci]

        @pl.when(jnp.logical_not(here))
        def _():
            send(RD1, gd.at[:, zi, :, ci], rd1.at[z], target)

    for i in (1, 3, 2):
        at, target = across_x(i)
        send(RA1, ga.at[at], ra1.at[i - 1], target)
    loop(0, 8, send_d1)

    first_half, second_half = pl.ds(0, 512), pl.ds(512, 512)
    arrived(W_XOWN)
    same(W_C1, wfull.at[:, yh, c, :, first_half], other_core)
    arrived(W_Z2)
    arrived(W_S2)
    arrived(W_Y)
    same(W_C3, wfull.at[:, :, c, :, second_half], other_core)
    arrived(W_XSIB)
    same(W_C2, wfull.at[:, 1 - yh, c, :, first_half], other_core)
    arrived(W_C3)
    arrived(W_C1)
    arrived(W_C2)

    def matmul(i):
        value = wfull[pl.ds(2 * i, 2)].reshape(256, D)
        back[:, pl.ds(pl.multiple_of(256 * i, 256), 256)] = lax.dot_general(
            cot[...], value, (((1,), (1,)), ((), ())), preferred_element_type=F32
        )

    loop(0, 4, matmul)

    def backward(i, sums):
        r = pl.multiple_of(i * ROWS, ROWS)
        totals, ones, twos = [], [], []
        for j in range(8):
            g = spread(kb[KW, :, LANES[j]])
            unit = normed[pl.ds(r, ROWS), LANES[j]]
            value = back[pl.ds(r, ROWS), LANES[j]] * slope[pl.ds(r, ROWS), LANES[j]]
            totals.append(sums[j] + fold(value * unit))
            hidden = value * g
            bcw[j, pl.ds(r + 8, ROWS), :] = hidden
            ones.append(hidden)
            twos.append(hidden * unit)
        first = jnp.sum(add_up(ones), axis=1, keepdims=True) * (1.0 / D)
        second = jnp.sum(add_up(twos), axis=1, keepdims=True) * (1.0 / D)
        scale = inv[pl.ds(r, ROWS), :]
        for j in range(8):
            unit = normed[pl.ds(r, ROWS), LANES[j]]
            bcw[j, pl.ds(r + 8, ROWS), :] = scale * (
                bcw[j, pl.ds(r + 8, ROWS), :] - first - unit * second
            )
        return tuple(totals)

    sums = lax.fori_loop(
        0, FRAMES // ROWS, backward, tuple(jnp.zeros((8, 128), F32) for _ in range(8)), unroll=2
    )
    send(BACK_A, bcw.at[:, pl.ds(FRAMES, 8)], bcw.at[:, pl.ds(0, 8)], after)
    send(BACK_B, bcw.at[:, pl.ds(8, 8)], bcw.at[:, pl.ds(FRAMES + 8, 8)], before)

    for k in range(KW):
        tacc[k] = jnp.zeros((8, D), F32)

    def products(i):
        r = pl.multiple_of(i * 64, 64)
        for k in range(KW):
            inside = mask[k, pl.ds(r, 64), :]
            for j in range(8):
                tacc[k, :, LANES[j]] += fold(
                    bcw[j, pl.ds(r + 8, 64), :] * (xw[j, pl.ds(r + 4 + k, 64), :] * inside)
                )

    loop(0, FRAMES // 64, products)
    for k in range(KW):
        line = jnp.sum(tacc[k], axis=0, keepdims=True)
        for j in range(8):
            kp[2 * j + k // 5, k % 5 : k % 5 + 1, :] = line[:, LANES[j]]
    for j in range(8):
        kp[2 * j + 1, 4:5, :] = jnp.sum(sums[j], axis=0, keepdims=True)

    def send_k1(i):
        at, target = row(i)
        send(K1, kp.at[at], rk1.at[i - 1], target)

    loop(1, 16, send_k1)

    arrived(RA1)
    total = add_up([sa1[...]] + [ra1[i].astype(F32) for i in range(3)])
    total = jnp.swapaxes(total.reshape(4, 2, 2, 4, 8, 128), 2, 3).reshape(4, 2, 4, 16, 128)
    sa1[...] = total.reshape(FRAMES, 128)
    sb1[...] = total.astype(BF16)

    def send_a2(i):
        at, target = across_y(i)
        send(RA2, sb1.at[:, at >> 2, at & 3], ra2.at[i - 1], target)

    loop(1, 8, send_a2)

    arrived(RD1)
    sd1[...] = add_up([rd1[i].astype(F32) for i in range(8)])
    for i in (1, 3, 2):
        at, target = across_x(i)
        send(RD2, sd1.at[at], rd2.at[i - 1], target)

    arrived(K1)
    me = x * 8 + z
    rk2[me] = add_up([kp[2 * y + c]] + [rk1[i] for i in range(15)])
    loop(1, 32, lambda i: send(K2, rk2.at[me], rk2.at[me], plane(i)))

    arrived(BACK_A)
    arrived(BACK_B)

    def rows_out(i):
        r = pl.multiple_of(i * ROWS, ROWS)
        parts = conv(bcw, r, True)
        for j in range(8):
            out_rows[0, pl.ds(r, ROWS), LANES[j]] = parts[j].astype(BF16)

    def send_a3(t):
        zi, ci, here, target = owner(t)

        @pl.when(here)
        def _():
            ra3[z] = sa2[zi, ci]

        @pl.when(jnp.logical_not(here))
        def _():
            send(RA3, sa2.at[zi, ci], ra3.at[z], target)

    def send_d3(i):
        at, target = across_y(i)
        send(RD3, sd2.at[at >> 2, at & 3], rd3.at[i - 1], target)

    def result(t):
        @pl.when(t == 8)
        def _():
            arrived(RA2)
            for i in range(4):
                own_rows = pl.ds(pl.multiple_of(128 * i + 64 * yh + 16 * yl, 16), 16)
                pieces = [sa1[own_rows, :]] + [ra2[k, i].astype(F32) for k in range(7)]
                sa2[i] = add_up(pieces).reshape(2, 8, 128)

            loop(0, 8, send_a3)
            arrived(RD2)
            sd2[...] = add_up([sd1[x], rd2[0], rd2[1], rd2[2]]).reshape(2, 4, 8, 128)

            loop(1, 8, send_d3)

        rows_out(t)

    loop(0, 16, result)

    arrived(K2)
    own = 2 * y + c
    kfull[own] = add_up([rk2[i] for i in range(32)])
    loop(1, 16, lambda i: send(K3, kfull.at[own], kfull.at[own], row(i)[1]))

    arrived(RA3)
    final[:, 0:128] = add_up([ra3[i] for i in range(8)])
    arrived(RD3)
    final[:, 128:256] = add_up([sd2[yh, yl]] + [rd3[i] for i in range(7)])
    gathered[dp] = final[...]
    loop(1, 16, lambda i: send(GATHER, final, gathered.at[dp], streams(i)))

    arrived(K3)
    for j in range(8):
        out_kernel[0:5, LANES[j]] = kfull[2 * j]
        out_kernel[5:9, LANES[j]] = kfull[2 * j + 1, 0:4]
        out_gain[0:1, LANES[j]] = kfull[2 * j + 1, 4:5]
    arrived(GATHER)
    for a in range(4):
        for b in range(4):
            out_weight[8 * a : 8 * a + 8, 256 * b : 256 * b + 256] = gathered[4 * a + b]

    for group in sorted(started):
        sent(group)


def hand_over(*refs):
    copies = [pltpu.make_async_copy(refs[i], refs[4 + i], refs[8].at[i]) for i in range(4)]
    for one in copies:
        one.start()
    for one in copies:
        one.wait()


def body(gated, cotangent, lengths, taps, gain, weight):
    v = pltpu.VMEM
    vmem, hbm = pl.BlockSpec(memory_space=v), pl.BlockSpec(memory_space=pltpu.HBM)
    rows, dweight, dkernel, dgain = pl.pallas_call(
        kernel,
        out_shape=(
            v((1, FRAMES, D), BF16),
            v((32, D), F32),
            v((KW, D), F32),
            v((1, D), F32),
        ),
        in_specs=[hbm] * 6,
        out_specs=(vmem,) * 4,
        scratch_shapes=[
            v((FRAMES, D), BF16),
            v((FRAMES, D), BF16),
            v((FRAMES, D), BF16),
            v((2, 16, D), BF16),
            v((16, D), BF16),
            v((8, FRAMES + 16, 128), F32),
            v((FRAMES + 16, 128), jnp.int32),
            v((KW, FRAMES, 128), F32),
            v((KW + 1, 8, D), F32),
            v((FRAMES, D), F32),
            v((FRAMES, D), F32),
            v((FRAMES, 128), F32),
            v((2, FRAMES, 512), BF16),
            v((FRAMES, 512), BF16),
            v((8, 2, 2, 32, D), BF16),
            v((FRAMES, D), F32),
            v((8, FRAMES + 16, 128), F32),
            v((KW, 8, D), F32),
            v((4, FRAMES, 128), BF16),
            v((4, 4, 2, 2, 32, 128), BF16),
            v((FRAMES, 128), F32),
            v((4, 2, 4, 16, 128), BF16),
            v((3, FRAMES, 128), BF16),
            v((7, 4, 16, 128), BF16),
            v((4, 2, 8, 128), F32),
            v((8, 8, 128), F32),
            v((8, 4, 2, 32, 128), BF16),
            v((4, 2, 32, 128), F32),
            v((3, 2, 32, 128), F32),
            v((2, 4, 8, 128), F32),
            v((7, 8, 128), F32),
            v((8, 256), F32),
            v((16, 8, 256), F32),
            v((16, 5, 128), F32),
            v((15, 5, 128), F32),
            v((32, 5, 128), F32),
            v((16, 5, 128), F32),
            pltpu.SMEM((1, 8), jnp.int32),
            v((KW, D), F32),
            v((1, D), F32),
            pltpu.SemaphoreType.DMA((8,)),
            pltpu.SemaphoreType.DMA((32,)),
            pltpu.SemaphoreType.DMA((32,)),
        ],
        compiler_params=pltpu.CompilerParams(
            collective_id=1, has_side_effects=True, vmem_limit_bytes=60 << 20
        ),
    )(gated, cotangent, lengths, taps, gain.reshape(1, D), weight)
    results = (rows, dweight, dkernel, dgain)
    rows, dweight, dkernel, dgain = pl.pallas_call(
        hand_over,
        out_shape=tuple(jax.ShapeDtypeStruct(r.shape, r.dtype) for r in results),
        in_specs=[vmem] * 4,
        out_specs=(hbm,) * 4,
        scratch_shapes=[pltpu.SemaphoreType.DMA((4,))],
        compiler_params=pltpu.CompilerParams(vmem_limit_bytes=32 << 20),
    )(*results)
    return rows, dweight, dkernel, dgain.reshape(D)


def solution(mesh):
    return jax.shard_map(
        body,
        mesh=mesh,
        in_specs=(
            P("dp", "seq", None),
            P("dp", "seq", None),
            P("dp", None),
            P(),
            P(),
            P("seq", None),
        ),
        out_specs=(P("dp", "seq", None), P("seq", None), P(), P()),
        check_vma=False,
    )
```
